256 devices in a mesh: replica: 4 (over y), context: 32 (over x, z), tensor: 2 (over core).
Axes of the slice: x: 4, y: 4, z: 8, core: 2. Of those that a mesh axis runs over, the one named last changes fastest.
Arguments:
- query_nope: bfloat16 [4, 2, 4, 128, 128], P('replica', None, None, 'tensor'), may hold values from -9 to 9
- query_rope: bfloat16 [4, 2, 4, 128, 64], P('replica', None, None, 'tensor'), may hold values from -72 to 72
- key_map: bfloat16 [128, 512, 128], P('tensor', ('replica', 'context')), may hold values from -0.5 to 0.5
- value_map: bfloat16 [128, 512, 128], P('tensor', ('replica', 'context')), may hold values from -1.5 to 1.5
- out_map: bfloat16 [7168, 2, 64, 128], P(None, 'tensor', 'context'), may hold values from -0.09375 to 0.09375
- prompt_latent: bfloat16 [4, 131072, 512], P('replica', 'context'), may hold values from -6 to 6
- prompt_rope: bfloat16 [4, 64, 131072], P('replica', None, 'context'), may hold values from -6 to 6
- prompt_lengths: int32 [4], P('replica'), may hold values from 65536 to 131072, as said below
- suffix_latent: bfloat16 [4, 4, 128, 512], P('replica'), may hold values from -9 to 9
- suffix_rope: bfloat16 [4, 4, 64, 128], P('replica'), may hold values from -9 to 9
- suffix_lengths: int32 [4, 4], P('replica'), may hold values from 1 to 128, as said below
- new_latent: bfloat16 [4, 2, 4, 512], P('replica'), may hold values from -12 to 12
- new_rope: bfloat16 [4, 2, 4, 64], P('replica'), may hold values from -12 to 12
Outputs:
- mixed: bfloat16 [4, 7168, 2, 4], P('replica', ('context', 'tensor'))
The draws below stay inside these ranges and needn't reach their ends.
Inputs may be any that keep to these rules, and one draw needn't show every extreme that they name: `prompt_lengths`: some prompt has all 131072 positions. `suffix_lengths`: some sample fills all 128 slots.
All inputs are finite; a program needn't handle non-finite values.
Results may differ from the reference program's by a relative error of at most 0.017.
Values may be sent and summed in bfloat16 or wider, within the bound.
A program may use at most 128 MiB of HBM per device.

```python
import jax
import jax.numpy as jnp
from jax import lax

WIDTH = 7168
HEADS = 128
LAT = 512
NOPE = 128
ROPE = 64
VDIM = 128
PROMPT_DEV = 4096
SAMPLES = 4
SUFFIX = 128
STEPS = 2
PROMPTS = 4
PROMPT = 131072
N_CONTEXT = 32
N_TENSOR = 2


def draw_query_nope(key, part):
    key = jax.random.fold_in(key, 3)
    drawn_rows = jnp.clip(1.5 * jax.random.normal(key, (PROMPTS, STEPS, SAMPLES, HEADS, NOPE), jnp.float32), -9.0, 9.0)
    return drawn_rows.astype(jnp.bfloat16)


def draw_query_rope(key, part):
    key = jax.random.fold_in(key, 7)
    drawn_rows = jnp.clip(jax.random.normal(key, (PROMPTS, STEPS, SAMPLES, HEADS, ROPE), jnp.float32), -6.0, 6.0)
    return drawn_rows.astype(jnp.bfloat16)


def draw_prompt_rope(key, part):
    key = jax.random.fold_in(key, 9)
    drawn_keys = jnp.clip(jax.random.normal(key, (PROMPTS, ROPE, PROMPT), jnp.float32), -6.0, 6.0)
    return drawn_keys.astype(jnp.bfloat16)


def draw_prompt_lengths(key, part):
    key = jax.random.fold_in(key, 5)
    length_key, choose_key = jax.random.split(key)
    drawn_lengths = jax.random.randint(length_key, (PROMPTS,), PROMPT // 2, PROMPT + 1)
    longest = jax.random.randint(choose_key, (), 0, PROMPTS)
    return jnp.where(jnp.arange(PROMPTS) == longest, PROMPT, drawn_lengths).astype(jnp.int32)


def draw_suffix_lengths(key, part):
    key = jax.random.fold_in(key, 13)
    length_key, choose_key = jax.random.split(key)
    drawn_lengths = jax.random.randint(length_key, (PROMPTS * SAMPLES,), 1, SUFFIX + 1)
    longest = jax.random.randint(choose_key, (), 0, PROMPTS * SAMPLES)
    filled = jnp.where(jnp.arange(PROMPTS * SAMPLES) == longest, SUFFIX, drawn_lengths)
    return filled.reshape(PROMPTS, SAMPLES).astype(jnp.int32)


def level_of(key, extent, pieces, least, high):
    loudness, own = 1.0, jax.random.fold_in(key, 6)
    for position, parts in pieces:
        draws = jnp.exp(jax.random.uniform(jax.random.fold_in(own, position), (parts,), jnp.float32, least / len(pieces), high / len(pieces)))
        loudness = loudness * jnp.repeat(draws, extent[position] // parts).reshape([-1 if axis == position else 1 for axis in range(len(extent))])
    return loudness


def normal_values(rng, extent, scale, reach, cuts=(), held_as=jnp.bfloat16):
    factor_of = level_of(rng, extent, cuts, -0.22, 0.18) if cuts else 1.0
    result = jax.random.normal(rng, extent, jnp.float32) * scale * factor_of
    return jnp.minimum(jnp.maximum(result, -reach), reach).astype(held_as)


def setup_inputs(seed: int = 0) -> dict:
    seeds = jax.random.split(jax.random.key(seed), 14)
    return {
        "query_nope": draw_query_nope(jax.random.fold_in(seeds[13], 71), 0),
        "query_rope": draw_query_rope(jax.random.fold_in(seeds[13], 71), 0),
        "key_map": normal_values(seeds[2], (HEADS, LAT, NOPE), NOPE ** -0.5, 0.5, ((0, 2), (1, 128))),
        "value_map": normal_values(seeds[3], (HEADS, LAT, VDIM), 0.25, 1.5, ((0, 2), (1, 128))),
        "out_map": normal_values(seeds[4], (WIDTH, N_TENSOR, HEADS // N_TENSOR, VDIM), (HEADS * VDIM // 4) ** -0.5, 0.09375, ((1, 2), (2, 32))),
        "prompt_latent": normal_values(seeds[5], (PROMPTS, PROMPT, LAT), 1.0, 6.0, ((0, 4), (1, 32))),
        "prompt_rope": draw_prompt_rope(jax.random.fold_in(seeds[13], 71), 0),
        "prompt_lengths": draw_prompt_lengths(jax.random.fold_in(seeds[13], 71), 0),
        "suffix_latent": normal_values(seeds[8], (PROMPTS, SAMPLES, SUFFIX, LAT), 1.5, 9.0, ((0, 4),)),
        "suffix_rope": normal_values(seeds[9], (PROMPTS, SAMPLES, ROPE, SUFFIX), 1.5, 9.0, ((0, 4),)),
        "suffix_lengths": draw_suffix_lengths(jax.random.fold_in(seeds[13], 71), 0),
        "new_latent": normal_values(seeds[11], (PROMPTS, STEPS, SAMPLES, LAT), 2.0, 12.0, ((0, 4),)),
        "new_rope": normal_values(seeds[12], (PROMPTS, STEPS, SAMPLES, ROPE), 2.0, 12.0, ((0, 4),)),
    }


masked_score = -1.0e30


def block_part(lat_rows, rope_rows, keys_here, rope_here, valid_keys, scaling):
    scores = lax.dot_general(lat_rows, keys_here, (((1,), (1,)), ((), ())), preferred_element_type=jnp.float32)
    scores = (scores + jnp.dot(rope_rows, rope_here, preferred_element_type=jnp.float32)) * scaling
    scores = jnp.where(valid_keys[None, :], scores, masked_score)
    row_max = jnp.max(scores, axis=1)
    exponent = jnp.where(valid_keys[None, :], jnp.exp(scores - row_max[:, None]), 0.0)
    row_sum = jnp.sum(exponent, axis=1)
    weighted = jnp.dot(exponent.astype(jnp.bfloat16), keys_here, preferred_element_type=jnp.float32)
    return row_max, row_sum, weighted


def join(former, latter):
    row_max = jnp.maximum(former[0], latter[0])
    former_scale = jnp.exp(former[0] - row_max)
    latter_scale = jnp.exp(latter[0] - row_max)
    return (row_max, former[1] * former_scale + latter[1] * latter_scale,
            former[2] * former_scale[..., None] + latter[2] * latter_scale[..., None])


def recent_part(latent_q, rope_q, suffix_keys, suffix_rot, suffix_len, new_keys, new_rot, scaling):
    latent_wide = latent_q.astype(jnp.float32)
    rope_wide = rope_q.astype(jnp.float32)
    suffix_scores = jnp.einsum("tshl,sil->tshi", latent_wide, suffix_keys.astype(jnp.float32))
    suffix_scores = (suffix_scores + jnp.einsum("tshr,sri->tshi", rope_wide, suffix_rot.astype(jnp.float32))) * scaling
    new_scores = jnp.einsum("tshl,usl->tshu", latent_wide, new_keys.astype(jnp.float32))
    new_scores = (new_scores + jnp.einsum("tshr,usr->tshu", rope_wide, new_rot.astype(jnp.float32))) * scaling
    suffix_valid = (jnp.arange(suffix_keys.shape[1], dtype=jnp.int32)[None, :] < suffix_len[:, None])[None, :, None, :]
    step_ids = jnp.arange(new_keys.shape[0], dtype=jnp.int32)
    new_valid = (step_ids[None, :] <= step_ids[:, None])[:, None, None, :]
    suffix_scores = jnp.where(suffix_valid, suffix_scores, masked_score)
    new_scores = jnp.where(new_valid, new_scores, masked_score)
    row_max = jnp.maximum(jnp.max(suffix_scores, axis=3), jnp.max(new_scores, axis=3))
    suffix_exp = jnp.where(suffix_valid, jnp.exp(suffix_scores - row_max[..., None]), 0.0)
    new_exp = jnp.where(new_valid, jnp.exp(new_scores - row_max[..., None]), 0.0)
    row_sum = jnp.sum(suffix_exp, axis=3) + jnp.sum(new_exp, axis=3)
    suffix_round = lax.optimization_barrier(suffix_exp.astype(jnp.bfloat16)).astype(jnp.float32)
    new_round = lax.optimization_barrier(new_exp.astype(jnp.bfloat16)).astype(jnp.float32)
    weighted = jnp.einsum("tshi,sil->tshl", suffix_round, suffix_keys.astype(jnp.float32))
    weighted = weighted + jnp.einsum("tshu,usl->tshl", new_round, new_keys.astype(jnp.float32))
    return row_max, row_sum, weighted


def reference(query_nope, query_rope, key_map, value_map, out_map, prompt_latent, prompt_rope, prompt_lengths, suffix_latent, suffix_rope, suffix_lengths, new_latent, new_rope):
    scaling = (NOPE + ROPE) ** -0.5
    row_count = STEPS * SAMPLES * HEADS
    out_rows = out_map.reshape(WIDTH, HEADS * VDIM)

    def one_prompt(inputs):
        nope_q, rope_q, keys_all, rope_all, length, suffix_keys, suffix_rot, suffix_len, new_keys, new_rot = inputs
        latent_q = jnp.einsum("tshn,hln->tshl", nope_q.astype(jnp.float32), key_map.astype(jnp.float32)).astype(jnp.bfloat16)
        lat_rows = latent_q.reshape(row_count, LAT)
        rope_rows = rope_q.reshape(row_count, ROPE)
        key_blocks = keys_all.reshape(N_CONTEXT, PROMPT_DEV, LAT)
        rope_blocks = jnp.transpose(rope_all.reshape(ROPE, N_CONTEXT, PROMPT_DEV), (1, 0, 2))

        def absorb(running, block_items):
            keys_here, rope_here, block_index = block_items
            positions = block_index * PROMPT_DEV + jnp.arange(PROMPT_DEV, dtype=jnp.int32)
            partial_now = block_part(lat_rows, rope_rows, keys_here, rope_here, positions < length, scaling)
            return join(running, partial_now), None

        initial = (jnp.full((row_count,), masked_score, jnp.float32), jnp.zeros((row_count,), jnp.float32),
                   jnp.zeros((row_count, LAT), jnp.float32))
        prompt_part, unused = lax.scan(absorb, initial, (key_blocks, rope_blocks, jnp.arange(N_CONTEXT, dtype=jnp.int32)))
        shaped = (prompt_part[0].reshape(STEPS, SAMPLES, HEADS), prompt_part[1].reshape(STEPS, SAMPLES, HEADS),
                  prompt_part[2].reshape(STEPS, SAMPLES, HEADS, LAT))
        recent = recent_part(latent_q, rope_q, suffix_keys, suffix_rot, suffix_len, new_keys, new_rot, scaling)
        row_max, row_sum, weighted = join(shaped, recent)
        latent_out = (weighted / row_sum[..., None]).astype(jnp.bfloat16)
        head_out = jnp.einsum("tshl,hlv->tshv", latent_out.astype(jnp.float32), value_map.astype(jnp.float32)).astype(jnp.bfloat16)
        flat_heads = head_out.reshape(STEPS * SAMPLES, HEADS * VDIM)
        mixed_out = lax.dot_general(out_rows, flat_heads, (((1,), (1,)), ((), ())), preferred_element_type=jnp.float32)
        return mixed_out.astype(jnp.bfloat16).reshape(WIDTH, STEPS, SAMPLES)

    return lax.map(one_prompt, (query_nope, query_rope, prompt_latent, prompt_rope, prompt_lengths, suffix_latent, suffix_rope, suffix_lengths, new_latent, new_rope))
```

```python
import functools
import math

import jax
import jax.numpy as jnp
from jax import lax
from jax.experimental import pallas as pl
from jax.experimental.pallas import tpu as pltpu
from jax.sharding import PartitionSpec as P

MESH = pl.DeviceIdType.MESH
F32 = jnp.float32
BF16 = jnp.bfloat16
masked_score = -1e30

NY, NX, NZ = 4, 4, 8
LAT, NOPE, ROPE, VDIM = 512, 128, 64, 128
KEYS = 4096
ROWS = 512
GROUP = 128
WIDE = 640
FEATS = 112
SCALE2 = (NOPE + ROPE) ** -0.5 * math.log2(math.e)


def iota(shape, axis):
    return lax.broadcasted_iota(jnp.int32, shape, axis)


def dot(a, b, dims=((1,), (0,))):
    return lax.dot_general(a, b, (dims, ((), ())), preferred_element_type=F32)


def ones_where(mask):
    return jnp.where(mask, 1.0, 0.0).astype(BF16)


def split3(x):
    first = x.astype(BF16).astype(F32)
    second = (x - first).astype(BF16).astype(F32)
    return first, second, x - first - second


def pack_stats(top, total):
    lanes = iota((top.shape[0], 128), 1)
    packed = jnp.zeros((top.shape[0], 128), F32)
    for k, part in enumerate(split3(top) + split3(total)):
        packed = jnp.where(lanes == k, part, packed)
    return packed.astype(BF16)


def read_stats(packed):
    wide = packed.astype(F32)
    top = wide[:, 0:1] + wide[:, 1:2] + wide[:, 2:3]
    total = wide[:, 3:4] + wide[:, 4:5] + wide[:, 5:6]
    return top, total


def kernel(
    length_ref,
    suffix_length_ref,
    qn_hbm,
    qr_hbm,
    km_hbm,
    vm_hbm,
    om_hbm,
    keys_hbm,
    rope_hbm,
    sl_hbm,
    sr_hbm,
    nl_hbm,
    nr_hbm,
    out_ref,
    qn,
    qr,
    qnp,
    kmg,
    qslots,
    q,
    keys,
    kt,
    om,
    outs,
    v1,
    v3,
    vde,
    kr,
    sr,
    nl,
    nr,
    scores,
    fs,
    f1,
    f2s,
    f2,
    yb,
    yp,
    yx,
    yxs,
    yz,
    yzs,
    load_sem,
    b_send,
    b_recv,
    v_send,
    v_recv,
    dz_send,
    dz_recv,
    dx_send,
    dx_recv,
    f1_send,
    f1_recv,
    f2_send,
    f2_recv,
    h_send,
    h_recv,
):
    r = lax.axis_index("replica")
    c = lax.axis_index("context")
    t = lax.axis_index("tensor")
    x, z = c // NZ, c % NZ

    def at_y(o):
        return ((r + o) % NY, c, t)

    def at_x(o):
        return (r, ((x + o) % NX) * NZ + z, t)

    def at_z(o):
        return (r, x * NZ + (z + o) % NZ, t)

    other = (r, c, 1 - t)

    def remote(src, dst, send, recv, device):
        return pltpu.make_async_remote_copy(
            src_ref=src, dst_ref=dst, send_sem=send, recv_sem=recv, device_id=device, device_id_type=MESH
        )

    loads = [
        (qn_hbm, qn),
        (qr_hbm, qr),
        (km_hbm, kmg.at[r]),
        (vm_hbm.at[x], v1.at[x]),
        (keys_hbm, keys),
        (rope_hbm, kt.at[pl.ds(LAT, ROPE)]),
        (om_hbm, om),
        (sl_hbm, kr.at[pl.ds(0, 512)]),
        (sr_hbm, sr),
        (nl_hbm, nl),
        (nr_hbm, nr),
    ]
    copies = [pltpu.make_async_copy(a, b, load_sem.at[i]) for i, (a, b) in enumerate(loads)]
    for copy in copies:
        copy.start()

    barrier = pltpu.get_barrier_semaphore()
    peers = [at_y(o) for o in range(1, NY)] + [at_x(o) for o in range(1, NX)]
    peers += [at_z(o) for o in range(1, NZ)] + [other]
    for peer in peers:
        pl.semaphore_signal(barrier, inc=1, device_id=peer, device_id_type=MESH)
    pl.semaphore_wait(barrier, len(peers))

    sends = []

    def go(copy):
        copy.start()
        sends.append(copy)
        return copy

    b_copies = [go(remote(km_hbm, kmg.at[r], b_send.at[o], b_recv.at[o], at_y(o))) for o in range(1, NY)]
    va_copies = [
        go(remote(vm_hbm.at[(x + o) % NX], v1.at[x], v_send.at[o], v_recv.at[o], at_x(o))) for o in range(1, NX)
    ]

    copies[0].wait()
    copies[1].wait()
    order = ones_where(
        (iota((ROWS, ROWS), 0) // 8 == iota((ROWS, ROWS), 1) % 64)
        & (iota((ROWS, ROWS), 0) % 8 == iota((ROWS, ROWS), 1) // 64)
    )
    qnp[...] = dot(order, qn[...]).astype(BF16)
    widen = ones_where(iota((ROPE, 128), 0) == iota((ROPE, 128), 1))
    rope_rows = dot(order, dot(qr[...], widen).astype(BF16))
    q[:, LAT:WIDE] = jnp.where(iota((ROWS, 128), 1) == ROPE, 1.0, rope_rows).astype(BF16)

    position = c * KEYS + iota((64, KEYS), 1)
    beyond = (position >= length_ref[0]) & (iota((64, KEYS), 0) == 0)
    kt[LAT + ROPE : WIDE, :] = jnp.where(beyond, masked_score, 0.0).astype(BF16)
    copies[4].wait()

    @pl.loop(0, KEYS // 512)
    def _(i):
        rows = pl.ds(pl.multiple_of(i * 512, 512), 512)
        kt[0:LAT, rows] = keys[rows, :].T

    copies[5].wait()

    copies[2].wait()
    for copy in b_copies:
        copy.wait_recv()
    absorbed = dot(kmg[...].reshape(1024, NOPE), qnp[...], ((1,), (1,)))
    own_head = (iota((1024, ROWS), 0) // 4) % 64 == iota((1024, ROWS), 1) // 8
    absorbed = jnp.where(own_head, absorbed, 0.0).astype(BF16)
    pick = ones_where(
        (iota((16, 1024), 1) // 256 == iota((16, 1024), 0) // 4) & (iota((16, 1024), 1) % 4 == iota((16, 1024), 0) % 4)
    )
    qslots[c] = dot(pick, absorbed).astype(BF16)

    dz_copies = [
        go(remote(qslots.at[c], qslots.at[c], dz_send.at[o], dz_recv.at[o], at_z(o))) for o in range(1, NZ)
    ]
    dx_copies = []
    for i in range(NZ):
        if i:
            dz_copies[i - 1].wait_recv()
        slot = x * NZ + (z - i + NZ) % NZ
        for o in range(1, NX):
            k = i * 3 + o - 1
            dx_copies.append(go(remote(qslots.at[slot], qslots.at[slot], dx_send.at[k], dx_recv.at[k], at_x(o))))

    copies[3].wait()
    for copy in va_copies:
        copy.wait_recv()
    v3[r, :, z] = v1[:, z]
    vb_copies = [
        go(remote(v1.at[:, (z + o) % NZ], v3.at[r, :, z], v_send.at[3 + o], v_recv.at[3 + o], at_z(o)))
        for o in range(1, NZ)
    ]

    copies[6].wait()
    apart = ones_where(iota((256, 224), 1) == (iota((256, 224), 0) % 128) * 2 + iota((256, 224), 0) // 128)
    apart = jnp.where(iota((256, 224), 0) % 128 < FEATS, apart, jnp.zeros_like(apart))

    @pl.loop(0, 64)
    def _(d):
        both = dot(apart, om[d]).astype(BF16)
        outs[d, :, 0:128] = both[0:128]
        outs[d, :, 128:256] = both[128:256]

    for copy in vb_copies:
        copy.wait_recv()
    vc_copies = [
        go(remote(v3.at[r], v3.at[r], v_send.at[10 + o], v_recv.at[10 + o], at_y(o))) for o in range(1, NY)
    ]

    for copy in dx_copies:
        copy.wait_recv()
    row_of = iota((LAT, LAT), 0)
    line_up = ones_where(((row_of // 4) % 4) * 128 + (row_of // 16) * 4 + row_of % 4 == iota((LAT, LAT), 1))
    q[:, 0:LAT] = dot(qslots[...].reshape(LAT, ROWS), line_up, ((0,), (0,))).astype(BF16)

    f1_copies = []
    for i, o in enumerate((2, 1, 3, 0)):
        g = (x + o) % NX
        rows = pl.ds(pl.multiple_of(g * GROUP, GROUP), GROUP)
        q_rows = q[rows, :]
        top = None
        for k in range(KEYS // 512):
            cols = slice(k * 512, (k + 1) * 512)
            part = dot(q_rows, kt[:, cols])
            scores[:, cols] = part
            here = jnp.maximum(
                jnp.maximum(part[:, 0:128], part[:, 128:256]), jnp.maximum(part[:, 256:384], part[:, 384:512])
            )
            top = here if top is None else jnp.maximum(top, here)
        top = jnp.max(top, axis=1, keepdims=True)
        total = jnp.zeros((GROUP, 128), F32)
        weighted = jnp.zeros((GROUP, LAT), F32)
        for k in range(KEYS // 512):
            cols = slice(k * 512, (k + 1) * 512)
            e = jnp.exp2((scores[:, cols] - top) * SCALE2)
            total += e[:, 0:128] + e[:, 128:256] + e[:, 256:384] + e[:, 384:512]
            weighted += dot(e.astype(BF16), keys[cols, :])
        total = jnp.sum(total, axis=1, keepdims=True)
        if o:
            fs[i, :, 0:LAT] = weighted.astype(BF16)
            fs[i, :, LAT:WIDE] = pack_stats(top, total)
            f1_copies.append(go(remote(fs.at[i], f1.at[x], f1_send.at[i], f1_recv.at[i], at_x(o))))
        else:
            f1[x, :, 0:LAT] = weighted.astype(BF16)
            f1[x, :, LAT:WIDE] = pack_stats(top, total)

    for copy in f1_copies:
        copy.wait_recv()
    stats = [read_stats(f1[k, :, LAT:WIDE]) for k in range(NX)]
    top = functools.reduce(jnp.maximum, [s[0] for s in stats])
    factors = [jnp.exp2((s[0] - top) * SCALE2) for s in stats]
    total = sum(f * s[1] for f, s in zip(factors, stats))
    weighted = sum(f * f1[k, :, 0:LAT].astype(F32) for k, f in enumerate(factors))
    f2s[:, :, 0:LAT] = weighted.astype(BF16).reshape(NZ, 16, LAT)
    f2s[:, :, LAT:WIDE] = pack_stats(top, total).reshape(NZ, 16, 128)
    f2[z] = f2s[z]
    f2_copies = [
        go(remote(f2s.at[(z + o) % NZ], f2.at[z], f2_send.at[o], f2_recv.at[o], at_z(o))) for o in range(1, NZ)
    ]

    for i in (7, 8, 9, 10):
        copies[i].wait()
    place = ones_where(iota((128, 8), 0) == iota((128, 8), 1))
    kr[512:640, :] = dot(place, nl[...]).astype(BF16)
    new_rot = dot(place, nr[...]).astype(BF16)
    own = pl.ds(pl.multiple_of(c * 16, 16), 16)
    q_lat, q_rot = q[own, 0:LAT], q[own, LAT : LAT + ROPE]
    rot_scores = [dot(q_rot, sr[s]) for s in range(4)] + [dot(q_rot, new_rot, ((1,), (1,)))]
    recent = dot(q_lat, kr[...], ((1,), (1,))) + jnp.concatenate(rot_scores, axis=1)
    row, col = iota((16, WIDE), 0), iota((16, WIDE), 1)
    limit = jnp.zeros((16, WIDE), jnp.int32)
    for s in range(4):
        limit = jnp.where(col // 128 == s, suffix_length_ref[0, s], limit)
    suffix_valid = (col < 512) & (col // 128 == row % 4) & (col % 128 < limit)
    fresh = col - 512
    new_valid = (fresh >= 0) & (fresh < 8) & (fresh % 4 == row % 4) & (fresh // 4 <= (row // 4) % 2)
    valid = suffix_valid | new_valid
    recent = jnp.where(valid, recent, masked_score)
    recent_top = jnp.max(recent, axis=1, keepdims=True)
    e = jnp.where(valid, jnp.exp2((recent - recent_top) * SCALE2), 0.0)
    recent_total = jnp.sum(e, axis=1, keepdims=True)
    recent_sum = dot(e.astype(BF16), kr[...])

    for copy in vc_copies:
        copy.wait_recv()
    flat = v3[...].reshape(1024, VDIM)
    for k in range(2):
        latent = iota((LAT, 1024), 0)
        pick = ones_where(iota((LAT, 1024), 1) == (latent // 4) * 8 + k * 4 + latent % 4)
        vde[:, k * 128 : (k + 1) * 128] = dot(pick, flat).astype(BF16)

    for copy in f2_copies:
        copy.wait_recv()
    stats = [read_stats(f2[k, :, LAT:WIDE]) for k in range(NZ)]
    top = functools.reduce(jnp.maximum, [s[0] for s in stats] + [recent_top])
    factors = [jnp.exp2((s[0] - top) * SCALE2) for s in stats]
    recent_factor = jnp.exp2((recent_top - top) * SCALE2)
    total = sum(f * s[1] for f, s in zip(factors, stats)) + recent_factor * recent_total
    weighted = sum(f * f2[k, :, 0:LAT].astype(F32) for k, f in enumerate(factors)) + recent_factor * recent_sum
    latent_out = (weighted / total).astype(BF16)

    head_out = dot(latent_out, vde[...])
    head_out = jnp.concatenate([head_out[0:8, 0:128], head_out[8:16, 128:256]], axis=1).astype(BF16)
    for d in range(64):
        yb[d % 2, d // 2] = dot(head_out, outs[d], ((1,), (1,)))

    pair = go(remote(yb.at[1 - t], yp, h_send.at[0], h_recv.at[0], other))
    pair.wait_recv()
    yxs[...] = (yb[t] + yp[...]).reshape(NX, NZ, 8, 128)
    yx[x] = yxs[x]
    hx_copies = [
        go(remote(yxs.at[(x + o) % NX], yx.at[x], h_send.at[o], h_recv.at[o], at_x(o))) for o in range(1, NX)
    ]
    for copy in hx_copies:
        copy.wait_recv()
    yzs[...] = yx[0] + yx[1] + yx[2] + yx[3]
    yz[z] = yzs[z]
    hz_copies = [
        go(remote(yzs.at[(z + o) % NZ], yz.at[z], h_send.at[3 + o], h_recv.at[3 + o], at_z(o))) for o in range(1, NZ)
    ]
    for copy in hz_copies:
        copy.wait_recv()
    out_ref[...] = jnp.sum(yz[...], axis=0)

    for copy in sends:
        copy.wait_send()


def shards(
    query_nope,
    query_rope,
    key_map,
    value_map,
    out_map,
    prompt_latent,
    prompt_rope,
    prompt_lengths,
    suffix_latent,
    suffix_rope,
    suffix_lengths,
    new_latent,
    new_rope,
):
    any_spec = pl.BlockSpec(memory_space=pl.ANY)
    smem_spec = pl.BlockSpec(memory_space=pltpu.SMEM)
    dma = pltpu.SemaphoreType.DMA
    vmem = pltpu.VMEM
    summed = pl.pallas_call(
        kernel,
        out_shape=jax.ShapeDtypeStruct((8, 128), F32),
        in_specs=[smem_spec] * 2 + [any_spec] * 11,
        out_specs=pl.BlockSpec(memory_space=pltpu.VMEM),
        scratch_shapes=[
            vmem((ROWS, NOPE), BF16),
            vmem((ROWS, ROPE), BF16),
            vmem((ROWS, NOPE), BF16),
            vmem((NY, 256, NOPE), BF16),
            vmem((NX * NZ, 16, ROWS), BF16),
            vmem((ROWS, WIDE), BF16),
            vmem((KEYS, LAT), BF16),
            vmem((WIDE, KEYS), BF16),
            vmem((64, 224, VDIM), BF16),
            vmem((64, 128, 256), BF16),
            vmem((NX, NZ, 8, VDIM), BF16),
            vmem((NY, NX, NZ, 8, VDIM), BF16),
            vmem((LAT, 256), BF16),
            vmem((WIDE, LAT), BF16),
            vmem((4, ROPE, 128), BF16),
            vmem((8, LAT), BF16),
            vmem((8, ROPE), BF16),
            vmem((GROUP, KEYS), F32),
            vmem((3, GROUP, WIDE), BF16),
            vmem((NX, GROUP, WIDE), BF16),
            vmem((NZ, 16, WIDE), BF16),
            vmem((NZ, 16, WIDE), BF16),
            vmem((2, NX * NZ, 8, 128), F32),
            vmem((NX * NZ, 8, 128), F32),
            vmem((NX, NZ, 8, 128), F32),
            vmem((NX, NZ, 8, 128), F32),
            vmem((NZ, 8, 128), F32),
            vmem((NZ, 8, 128), F32),
            dma((11,)),
            dma((NY,)),
            dma((NY,)),
            dma((14,)),
            dma((14,)),
            dma((NZ,)),
            dma((NZ,)),
            dma((24,)),
            dma((24,)),
            dma((3,)),
            dma((3,)),
            dma((NZ,)),
            dma((NZ,)),
            dma((11,)),
            dma((11,)),
        ],
        compiler_params=pltpu.CompilerParams(
            collective_id=0, has_side_effects=True, vmem_limit_bytes=56 * 1024 * 1024
        ),
        name="latent_attention",
    )(
        prompt_lengths,
        suffix_lengths,
        query_nope.reshape(ROWS, NOPE),
        query_rope.reshape(ROWS, ROPE),
        key_map.reshape(256, NOPE),
        value_map.reshape(NX, NZ, 8, VDIM),
        out_map.reshape(64, 224, VDIM),
        prompt_latent[0],
        prompt_rope[0],
        suffix_latent.reshape(512, LAT),
        suffix_rope[0],
        new_latent.reshape(8, LAT),
        new_rope.reshape(8, ROPE),
    )
    return summed[:, :FEATS].T.astype(BF16).reshape(1, FEATS, 2, 4)


def solution(mesh):
    placed = (
        P("replica", None, None, "tensor", None),
        P("replica", None, None, "tensor", None),
        P("tensor", ("replica", "context"), None),
        P("tensor", ("replica", "context"), None),
        P(None, "tensor", "context", None),
        P("replica", "context", None),
        P("replica", None, "context"),
        P("replica"),
        P("replica", None, None, None),
        P("replica", None, None, None),
        P("replica", None),
        P("replica", None, None, None),
        P("replica", None, None, None),
    )
    return jax.shard_map(
        shards,
        mesh=mesh,
        in_specs=placed,
        out_specs=P("replica", ("context", "tensor"), None, None),
        check_vma=False,
    )
```

```python
import functools
import math

import jax
import jax.numpy as jnp
from jax import lax
from jax.experimental import pallas as pl
from jax.experimental.pallas import tpu as pltpu
from jax.sharding import PartitionSpec as P

MESH = pl.DeviceIdType.MESH
F32 = jnp.float32
BF16 = jnp.bfloat16
masked_score = -1e30

NY, NX, NZ = 4, 4, 8
LAT, NOPE, ROPE, VDIM = 512, 128, 64, 128
KEYS = 4096
ROWS = 512
GROUP = 128
WIDE = 640
FEATS = 112
SCALE2 = (NOPE + ROPE) ** -0.5 * math.log2(math.e)


def iota(shape, axis):
    return lax.broadcasted_iota(jnp.int32, shape, axis)


def dot(a, b, dims=((1,), (0,))):
    return lax.dot_general(a, b, (dims, ((), ())), preferred_element_type=F32)


def ones_where(mask):
    return jnp.where(mask, 1.0, 0.0).astype(BF16)


def split3(x):
    first = x.astype(BF16).astype(F32)
    second = (x - first).astype(BF16).astype(F32)
    return first, second, x - first - second


def pack_stats(top, total):
    lanes = iota((top.shape[0], 128), 1)
    packed = jnp.zeros((top.shape[0], 128), F32)
    for k, part in enumerate(split3(top) + split3(total)):
        packed = jnp.where(lanes == k, part, packed)
    return packed.astype(BF16)


def read_stats(packed):
    wide = packed.astype(F32)
    top = wide[:, 0:1] + wide[:, 1:2] + wide[:, 2:3]
    total = wide[:, 3:4] + wide[:, 4:5] + wide[:, 5:6]
    return top, total


def kernel(
    length_ref,
    suffix_length_ref,
    qn_hbm,
    qr_hbm,
    km_hbm,
    vm_hbm,
    om_hbm,
    keys_hbm,
    rope_hbm,
    sl_hbm,
    sr_hbm,
    nl_hbm,
    nr_hbm,
    out_ref,
    qn,
    qr,
    qnp,
    kmg,
    qslots,
    q,
    keys,
    kt,
    om,
    outs,
    v1,
    v3,
    vde,
    kr,
    sr,
    nl,
    nr,
    scores,
    fs,
    f1,
    f2s,
    f2,
    yb,
    yx,
    yz,
    yzs,
    load_sem,
    b_send,
    b_recv,
    v_send,
    v_recv,
    dz_send,
    dz_recv,
    dx_send,
    dx_recv,
    f1_send,
    f1_recv,
    f2_send,
    f2_recv,
    h_send,
    h_recv,
):
    r = lax.axis_index("replica")
    c = lax.axis_index("context")
    t = lax.axis_index("tensor")
    x, z = c // NZ, c % NZ

    def at_y(o):
        return ((r + o) % NY, c, t)

    def at_x(o, core=t):
        return (r, ((x + o) % NX) * NZ + z, core)

    def at_z(o):
        return (r, x * NZ + (z + o) % NZ, t)

    def remote(src, dst, send, recv, device):
        return pltpu.make_async_remote_copy(
            src_ref=src, dst_ref=dst, send_sem=send, recv_sem=recv, device_id=device, device_id_type=MESH
        )

    loads = [
        (qn_hbm, qn),
        (qr_hbm, qr),
        (keys_hbm, keys),
        (om_hbm, om),
        (km_hbm, kmg.at[r]),
        (rope_hbm, kt.at[pl.ds(LAT, ROPE)]),
        (vm_hbm.at[x], v1.at[x]),
        (sl_hbm, kr.at[pl.ds(0, 512)]),
        (sr_hbm, sr),
        (nl_hbm, nl),
        (nr_hbm, nr),
    ]
    copies = [pltpu.make_async_copy(a, b, load_sem.at[i]) for i, (a, b) in enumerate(loads)]
    for copy in copies:
        copy.start()

    barrier = pltpu.get_barrier_semaphore()
    peers = [at_y(o) for o in range(1, NY)] + [at_x(o) for o in range(1, NX)]
    peers += [at_x(o, 1 - t) for o in range(NX)] + [at_z(o) for o in range(1, NZ)]
    for peer in peers:
        pl.semaphore_signal(barrier, inc=1, device_id=peer, device_id_type=MESH)

    copies[0].wait()
    copies[1].wait()
    order = ones_where(
        (iota((ROWS, ROWS), 0) // 8 == iota((ROWS, ROWS), 1) % 64)
        & (iota((ROWS, ROWS), 0) % 8 == iota((ROWS, ROWS), 1) // 64)
    )
    qnp[...] = dot(order, qn[...]).astype(BF16)
    widen = ones_where(iota((ROPE, 128), 0) == iota((ROPE, 128), 1))
    rope_rows = dot(order, dot(qr[...], widen).astype(BF16))
    q[:, LAT:WIDE] = jnp.where(iota((ROWS, 128), 1) == ROPE, 1.0, rope_rows).astype(BF16)

    position = c * KEYS + iota((64, KEYS), 1)
    beyond = (position >= length_ref[0]) & (iota((64, KEYS), 0) == 0)
    kt[LAT + ROPE : WIDE, :] = jnp.where(beyond, masked_score, 0.0).astype(BF16)
    copies[2].wait()

    @pl.loop(0, KEYS // 512)
    def _(i):
        rows = pl.ds(pl.multiple_of(i * 512, 512), 512)
        kt[0:LAT, rows] = keys[rows, :].T

    copies[3].wait()
    apart = ones_where(iota((256, 224), 1) == (iota((256, 224), 0) % 128) * 2 + iota((256, 224), 0) // 128)
    apart = jnp.where(iota((256, 224), 0) % 128 < FEATS, apart, jnp.zeros_like(apart))

    @pl.loop(0, 64, step=8)
    def _(first):
        for d in range(8):
            both = dot(apart, om[first + d]).astype(BF16)
            outs[first + d, :, 0:128] = both[0:128]
            outs[first + d, :, 128:256] = both[128:256]

    pl.semaphore_wait(barrier, len(peers))

    sends = []

    def go(copy):
        copy.start()
        sends.append(copy)
        return copy

    b_copies = [go(remote(km_hbm, kmg.at[r], b_send.at[o], b_recv.at[o], at_y(o))) for o in range(1, NY)]
    va_copies = [
        go(remote(vm_hbm.at[(x + o) % NX], v1.at[x], v_send.at[o], v_recv.at[o], at_x(o))) for o in range(1, NX)
    ]

    copies[4].wait()
    for copy in b_copies:
        copy.wait_recv()
    absorbed = dot(kmg[...].reshape(1024, NOPE), qnp[...], ((1,), (1,)))
    own_head = (iota((1024, ROWS), 0) // 4) % 64 == iota((1024, ROWS), 1) // 8
    absorbed = jnp.where(own_head, absorbed, 0.0).astype(BF16)
    pick = ones_where(
        (iota((16, 1024), 1) // 256 == iota((16, 1024), 0) // 4) & (iota((16, 1024), 1) % 4 == iota((16, 1024), 0) % 4)
    )
    piece = dot(pick, absorbed).astype(BF16)
    qslots[0, c] = piece[:, 0:256]
    qslots[1, c] = piece[:, 256:512]

    def slots(half, first, count=1):
        return qslots.at[half, pl.ds(first, count)]

    dz_copies = {
        o: go(
            remote(qslots.at[:, c], qslots.at[:, c], dz_send.at[o], dz_recv.at[o], at_z(o))
        )
        for o in (4, 3, 5, 2, 6, 1, 7)
    }
    early_copies, late_copies = [], []
    for k, i in enumerate((0, 1, 7, 2, 6, 3, 5, 4)):
        if i:
            dz_copies[i].wait_recv()
        slot = x * NZ + (z - i + NZ) % NZ
        for o in (2, 1, 3):
            half = 1 - ((x + o) % NX) // 2
            n = k * 3 + o - 1
            early_copies.append(
                go(remote(slots(half, slot), slots(half, slot), dx_send.at[n], dx_recv.at[n], at_x(o)))
            )
    for o in (2, 1, 3):
        half = ((x + o) % NX) // 2
        n = 23 + o
        late_copies.append(
            go(
                remote(
                    slots(half, x * NZ, NZ), slots(half, x * NZ, NZ), dx_send.at[n], dx_recv.at[n], at_x(o)
                )
            )
        )

    copies[6].wait()
    for copy in va_copies:
        copy.wait_recv()
    v3[r, :, z] = v1[:, z]
    vb_copies = [
        go(remote(v1.at[:, (z + o) % NZ], v3.at[r, :, z], v_send.at[3 + o], v_recv.at[3 + o], at_z(o)))
        for o in range(1, NZ)
    ]

    copies[5].wait()
    row_of = iota((LAT, LAT), 0)
    line_up = ones_where(((row_of // 4) % 4) * 128 + (row_of // 16) * 4 + row_of % 4 == iota((LAT, LAT), 1))
    f1_copies = []
    for i in range(NX):
        o = (2, 3 - 2 * (x % 2), 1 + 2 * (x % 2), 0)[i]
        if i % 2 == 0:
            for copy in (late_copies if i else early_copies):
                copy.wait_recv()
            half = x // 2 if i else 1 - x // 2
            gathered = dot(qslots[half].reshape(LAT, 256), line_up, ((0,), (0,)))
            q[pl.ds(pl.multiple_of(half * 256, 256), 256), 0:LAT] = gathered.astype(BF16)
        g = (x + o) % NX
        rows = pl.ds(pl.multiple_of(g * GROUP, GROUP), GROUP)
        q_rows = q[rows, :]
        top = None
        for k in range(KEYS // 512):
            cols = slice(k * 512, (k + 1) * 512)
            part = dot(q_rows, kt[:, cols])
            scores[:, cols] = part
            here = jnp.maximum(
                jnp.maximum(part[:, 0:128], part[:, 128:256]), jnp.maximum(part[:, 256:384], part[:, 384:512])
            )
            top = here if top is None else jnp.maximum(top, here)
        top = jnp.max(top, axis=1, keepdims=True)
        total = jnp.zeros((GROUP, 128), F32)
        weighted = jnp.zeros((GROUP, LAT), F32)
        for k in range(KEYS // 512):
            cols = slice(k * 512, (k + 1) * 512)
            e = jnp.exp2((scores[:, cols] - top) * SCALE2)
            total += e[:, 0:128] + e[:, 128:256] + e[:, 256:384] + e[:, 384:512]
            weighted += dot(e.astype(BF16), keys[cols, :])
        total = jnp.sum(total, axis=1, keepdims=True)
        if i < NX - 1:
            fs[i, :, 0:LAT] = weighted.astype(BF16)
            fs[i, :, LAT:WIDE] = pack_stats(top, total)
            f1_copies.append(go(remote(fs.at[i], f1.at[x], f1_send.at[o], f1_recv.at[o], at_x(o))))
        else:
            f1[x, :, 0:LAT] = weighted.astype(BF16)
            f1[x, :, LAT:WIDE] = pack_stats(top, total)
        if i == 1:
            for copy in vb_copies:
                copy.wait_recv()
            vc_copies = [
                go(remote(v3.at[r], v3.at[r], v_send.at[10 + o], v_recv.at[10 + o], at_y(o)))
                for o in range(1, NY)
            ]

    for copy in f1_copies:
        copy.wait_recv()
    f2_copies = []
    for o in (4, 3, 5, 2, 6, 1, 7, 0):
        there = (z + o) % NZ
        rows = pl.ds(pl.multiple_of(there * 16, 16), 16)
        stats = [read_stats(f1[k, rows, LAT:WIDE]) for k in range(NX)]
        top = functools.reduce(jnp.maximum, [s[0] for s in stats])
        factors = [jnp.exp2((s[0] - top) * SCALE2) for s in stats]
        total = sum(f * s[1] for f, s in zip(factors, stats))
        weighted = sum(f * f1[k, rows, 0:LAT].astype(F32) for k, f in enumerate(factors))
        place = f2s if o else f2
        place[there, :, 0:LAT] = weighted.astype(BF16)
        place[there, :, LAT:WIDE] = pack_stats(top, total)
        if o:
            f2_copies.append(go(remote(f2s.at[there], f2.at[z], f2_send.at[o], f2_recv.at[o], at_z(o))))

    for i in (7, 8, 9, 10):
        copies[i].wait()
    place = ones_where(iota((128, 8), 0) == iota((128, 8), 1))
    kr[512:640, :] = (dot(place[:, 0:4], nl[0]) + dot(place[:, 4:8], nl[1])).astype(BF16)
    new_rot = dot(place, nr[...]).astype(BF16)
    own = pl.ds(pl.multiple_of(c * 16, 16), 16)
    q_lat, q_rot = q[own, 0:LAT], q[own, LAT : LAT + ROPE]
    rot_scores = [dot(q_rot, sr[s]) for s in range(4)] + [dot(q_rot, new_rot, ((1,), (1,)))]
    recent = dot(q_lat, kr[...], ((1,), (1,))) + jnp.concatenate(rot_scores, axis=1)
    row, col = iota((16, WIDE), 0), iota((16, WIDE), 1)
    limit = jnp.zeros((16, WIDE), jnp.int32)
    for s in range(4):
        limit = jnp.where(col // 128 == s, suffix_length_ref[0, s], limit)
    suffix_valid = (col < 512) & (col // 128 == row % 4) & (col % 128 < limit)
    fresh = col - 512
    new_valid = (fresh >= 0) & (fresh < 8) & (fresh % 4 == row % 4) & (fresh // 4 <= (row // 4) % 2)
    valid = suffix_valid | new_valid
    recent = jnp.where(valid, recent, masked_score)
    recent_top = jnp.max(recent, axis=1, keepdims=True)
    e = jnp.where(valid, jnp.exp2((recent - recent_top) * SCALE2), 0.0)
    recent_total = jnp.sum(e, axis=1, keepdims=True)
    recent_sum = dot(e.astype(BF16), kr[...])

    for copy in vc_copies:
        copy.wait_recv()
    flat = v3[...].reshape(1024, VDIM)
    for k in range(2):
        latent = iota((LAT, 1024), 0)
        pick = ones_where(iota((LAT, 1024), 1) == (latent // 4) * 8 + k * 4 + latent % 4)
        vde[:, k * 128 : (k + 1) * 128] = dot(pick, flat).astype(BF16)

    for copy in f2_copies:
        copy.wait_recv()
    stats = [read_stats(f2[k, :, LAT:WIDE]) for k in range(NZ)]
    top = functools.reduce(jnp.maximum, [s[0] for s in stats] + [recent_top])
    factors = [jnp.exp2((s[0] - top) * SCALE2) for s in stats]
    recent_factor = jnp.exp2((recent_top - top) * SCALE2)
    total = sum(f * s[1] for f, s in zip(factors, stats)) + recent_factor * recent_total
    weighted = sum(f * f2[k, :, 0:LAT].astype(F32) for k, f in enumerate(factors)) + recent_factor * recent_sum
    latent_out = (weighted / total).astype(BF16)

    head_out = dot(latent_out, vde[...])
    head_out = jnp.concatenate([head_out[0:8, 0:128], head_out[8:16, 128:256]], axis=1).astype(BF16)
    hx_copies = []
    for o, away in ((2, 1), (2, 0), (1, 1), (1, 0), (3, 1), (3, 0), (0, 1), (0, 0)):
        there, core = (x + o) % NX, (t + away) % 2
        for k in range(0, NZ, 2):
            first = (there * NZ + k) * 2 + core
            part = [dot(head_out, outs[first + 2 * m], ((1,), (1,))) for m in range(2)]
            place = yb if o or away else yx
            place[there, core, k * 8 : k * 8 + 16] = jnp.concatenate(part, axis=0).astype(BF16)
        if o or away:
            n = o * 2 + away
            hx_copies.append(go(remote(yb.at[there, core], yx.at[x, t], h_send.at[n], h_recv.at[n], at_x(o, core))))
    for copy in hx_copies:
        copy.wait_recv()
    own_sum = sum(yx[k, core].astype(F32) for k in range(NX) for core in range(2))
    yzs[...] = own_sum.reshape(NZ, 8, 128)
    yz[z] = yzs[z]
    hz_copies = [
        go(remote(yzs.at[(z + o) % NZ], yz.at[z], h_send.at[7 + o], h_recv.at[7 + o], at_z(o)))
        for o in (4, 3, 5, 2, 6, 1, 7)
    ]
    for copy in hz_copies:
        copy.wait_recv()
    out_ref[...] = jnp.sum(yz[...], axis=0)

    for copy in sends:
        copy.wait_send()


def shards(
    query_nope,
    query_rope,
    key_map,
    value_map,
    out_map,
    prompt_latent,
    prompt_rope,
    prompt_lengths,
    suffix_latent,
    suffix_rope,
    suffix_lengths,
    new_latent,
    new_rope,
):
    any_spec = pl.BlockSpec(memory_space=pl.ANY)
    smem_spec = pl.BlockSpec(memory_space=pltpu.SMEM)
    dma = pltpu.SemaphoreType.DMA
    vmem = pltpu.VMEM
    summed = pl.pallas_call(
        kernel,
        out_shape=jax.ShapeDtypeStruct((8, 128), F32),
        in_specs=[smem_spec] * 2 + [any_spec] * 11,
        out_specs=pl.BlockSpec(memory_space=pltpu.VMEM),
        scratch_shapes=[
            vmem((ROWS, NOPE), BF16),
            vmem((ROWS, ROPE), BF16),
            vmem((ROWS, NOPE), BF16),
            vmem((NY, 256, NOPE), BF16),
            vmem((2, NX * NZ, 16, 256), BF16),
            vmem((ROWS, WIDE), BF16),
            vmem((KEYS, LAT), BF16),
            vmem((WIDE, KEYS), BF16),
            vmem((64, 224, VDIM), BF16),
            vmem((64, 128, 256), BF16),
            vmem((NX, NZ, 8, VDIM), BF16),
            vmem((NY, NX, NZ, 8, VDIM), BF16),
            vmem((LAT, 256), BF16),
            vmem((WIDE, LAT), BF16),
            vmem((4, ROPE, 128), BF16),
            vmem((2, 4, LAT), BF16),
            vmem((8, ROPE), BF16),
            vmem((GROUP, KEYS), F32),
            vmem((3, GROUP, WIDE), BF16),
            vmem((NX, GROUP, WIDE), BF16),
            vmem((NZ, 16, WIDE), BF16),
            vmem((NZ, 16, WIDE), BF16),
            vmem((NX, 2, NZ * 8, 128), BF16),
            vmem((NX, 2, NZ * 8, 128), BF16),
            vmem((NZ, 8, 128), F32),
            vmem((NZ, 8, 128), F32),
            dma((11,)),
            dma((NY,)),
            dma((NY,)),
            dma((14,)),
            dma((14,)),
            dma((NZ,)),
            dma((NZ,)),
            dma((27,)),
            dma((27,)),
            dma((NX,)),
            dma((NX,)),
            dma((NZ,)),
            dma((NZ,)),
            dma((15,)),
            dma((15,)),
        ],
        compiler_params=pltpu.CompilerParams(
            collective_id=0, has_side_effects=True, vmem_limit_bytes=56 * 1024 * 1024
        ),
        name="latent_attention",
    )(
        prompt_lengths,
        suffix_lengths,
        query_nope.reshape(ROWS, NOPE),
        query_rope.reshape(ROWS, ROPE),
        key_map.reshape(256, NOPE),
        value_map.reshape(NX, NZ, 8, VDIM),
        out_map.reshape(64, 224, VDIM),
        prompt_latent[0],
        prompt_rope[0],
        suffix_latent.reshape(512, LAT),
        suffix_rope[0],
        new_latent[0],
        new_rope.reshape(8, ROPE),
    )
    return summed[:, :FEATS].T.astype(BF16).reshape(1, FEATS, 2, 4)


def solution(mesh):
    placed = (
        P("replica", None, None, "tensor", None),
        P("replica", None, None, "tensor", None),
        P("tensor", ("replica", "context"), None),
        P("tensor", ("replica", "context"), None),
        P(None, "tensor", "context", None),
        P("replica", "context", None),
        P("replica", None, "context"),
        P("replica"),
        P("replica", None, None, None),
        P("replica", None, None, None),
        P("replica", None),
        P("replica", None, None, None),
        P("replica", None, None, None),
    )
    return jax.shard_map(
        shards,
        mesh=mesh,
        in_specs=placed,
        out_specs=P("replica", ("context", "tensor"), None, None),
        check_vma=False,
    )
```

```python
import functools
import math

import jax
import jax.numpy as jnp
from jax import lax
from jax.experimental import pallas as pl
from jax.experimental.pallas import tpu as pltpu
from jax.sharding import PartitionSpec as P

MESH = pl.DeviceIdType.MESH
F32 = jnp.float32
BF16 = jnp.bfloat16
masked_score = -1e30

NY, NX, NZ = 4, 4, 8
LAT, NOPE, ROPE, VDIM = 512, 128, 64, 128
KEYS = 4096
ROWS = 512
GROUP = 128
WIDE = 640
FEATS = 112
SCALE2 = (NOPE + ROPE) ** -0.5 * math.log2(math.e)


def iota(shape, axis):
    return lax.broadcasted_iota(jnp.int32, shape, axis)


def dot(a, b, dims=((1,), (0,))):
    return lax.dot_general(a, b, (dims, ((), ())), preferred_element_type=F32)


def ones_where(mask):
    return jnp.where(mask, 1.0, 0.0).astype(BF16)


def split3(x):
    first = x.astype(BF16).astype(F32)
    second = (x - first).astype(BF16).astype(F32)
    return first, second, x - first - second


def pack_stats(top, total):
    lanes = iota((top.shape[0], 128), 1)
    packed = jnp.zeros((top.shape[0], 128), F32)
    for k, part in enumerate(split3(top) + split3(total)):
        packed = jnp.where(lanes == k, part, packed)
    return packed.astype(BF16)


def read_stats(packed):
    wide = packed.astype(F32)
    top = wide[:, 0:1] + wide[:, 1:2] + wide[:, 2:3]
    total = wide[:, 3:4] + wide[:, 4:5] + wide[:, 5:6]
    return top, total


def kernel(
    length_hbm,
    suffix_length_hbm,
    qn_hbm,
    qr_hbm,
    km_hbm,
    vm_hbm,
    om_hbm,
    keys_hbm,
    rope_hbm,
    sl_hbm,
    sr_hbm,
    nl_hbm,
    nr_hbm,
    out_ref,
    qn,
    qr,
    qnp,
    kmg,
    qslots,
    q,
    keys,
    kt,
    om,
    outs,
    v1,
    v3,
    vde,
    kr,
    sr,
    nl,
    nr,
    scores,
    fs,
    f1,
    f2s,
    f2,
    yb,
    yx,
    yz,
    yzs,
    length_ref,
    suffix_length_ref,
    load_sem,
    b_send,
    b_recv,
    v_send,
    v_recv,
    dz_send,
    dz_recv,
    dx_send,
    dx_recv,
    f1_send,
    f1_recv,
    f2_send,
    f2_recv,
    h_send,
    h_recv,
):
    r = lax.axis_index("replica")
    c = lax.axis_index("context")
    t = lax.axis_index("tensor")
    x, z = c // NZ, c % NZ

    def at_y(o):
        return ((r + o) % NY, c, t)

    def at_x(o, core=t):
        return (r, ((x + o) % NX) * NZ + z, core)

    def at_z(o):
        return (r, x * NZ + (z + o) % NZ, t)

    def remote(src, dst, send, recv, device):
        return pltpu.make_async_remote_copy(
            src_ref=src, dst_ref=dst, send_sem=send, recv_sem=recv, device_id=device, device_id_type=MESH
        )

    loads = [
        (qn_hbm, qn),
        (qr_hbm, qr),
        (keys_hbm, keys),
        (om_hbm, om),
        (km_hbm, kmg.at[r]),
        (rope_hbm, kt.at[pl.ds(LAT, ROPE)]),
        (vm_hbm.at[x], v1.at[x]),
        (sl_hbm, kr.at[pl.ds(0, 512)]),
        (sr_hbm, sr),
        (nl_hbm, nl),
        (nr_hbm, nr),
        (length_hbm, length_ref),
        (suffix_length_hbm, suffix_length_ref),
    ]
    copies = [pltpu.make_async_copy(a, b, load_sem.at[i]) for i, (a, b) in enumerate(loads)]
    for copy in copies:
        copy.start()

    barrier = pltpu.get_barrier_semaphore()
    peers = [at_y(o) for o in range(1, NY)] + [at_x(o) for o in range(1, NX)]
    peers += [at_x(o, 1 - t) for o in range(NX)] + [at_z(o) for o in range(1, NZ)]
    for peer in peers:
        pl.semaphore_signal(barrier, inc=1, device_id=peer, device_id_type=MESH)

    pl.semaphore_wait(barrier, len(peers))

    sends = []

    def go(copy):
        copy.start()
        sends.append(copy)
        return copy

    copies[4].wait()
    b_copies = [go(remote(kmg.at[r], kmg.at[r], b_send.at[o], b_recv.at[o], at_y(o))) for o in range(1, NY)]
    va_copies = [
        go(remote(vm_hbm.at[(x + o) % NX], v1.at[x], v_send.at[o], v_recv.at[o], at_x(o))) for o in range(1, NX)
    ]

    copies[0].wait()
    copies[1].wait()
    order = ones_where(
        (iota((ROWS, ROWS), 0) // 8 == iota((ROWS, ROWS), 1) % 64)
        & (iota((ROWS, ROWS), 0) % 8 == iota((ROWS, ROWS), 1) // 64)
    )
    qnp[...] = dot(order, qn[...]).astype(BF16)
    widen = ones_where(iota((ROPE, 128), 0) == iota((ROPE, 128), 1))
    rope_rows = dot(order, dot(qr[...], widen).astype(BF16))
    q[:, LAT:WIDE] = jnp.where(iota((ROWS, 128), 1) == ROPE, 1.0, rope_rows).astype(BF16)

    copies[11].wait()
    position = c * KEYS + iota((64, KEYS), 1)
    beyond = (position >= length_ref[0]) & (iota((64, KEYS), 0) == 0)
    kt[LAT + ROPE : WIDE, :] = jnp.where(beyond, masked_score, 0.0).astype(BF16)
    copies[2].wait()

    @pl.loop(0, KEYS // 512)
    def _(i):
        rows = pl.ds(pl.multiple_of(i * 512, 512), 512)
        kt[0:LAT, rows] = keys[rows, :].T

    copies[6].wait()
    for copy in va_copies:
        copy.wait_recv()
    v3[r, :, z] = v1[:, z]
    vb_copies = [
        go(remote(v1.at[:, (z + o) % NZ], v3.at[r, :, z], v_send.at[3 + o], v_recv.at[3 + o], at_z(o)))
        for o in range(1, NZ)
    ]

    copies[3].wait()
    apart = ones_where(iota((256, 224), 1) == (iota((256, 224), 0) % 128) * 2 + iota((256, 224), 0) // 128)
    apart = jnp.where(iota((256, 224), 0) % 128 < FEATS, apart, jnp.zeros_like(apart))

    def take_apart(begin, end):
        @pl.loop(begin, end, step=8)
        def _(first):
            for d in range(8):
                both = dot(apart, om[first + d]).astype(BF16)
                outs[first + d, :, 0:128] = both[0:128]
                outs[first + d, :, 128:256] = both[128:256]

    take_apart(0, 24)

    for copy in b_copies:
        copy.wait_recv()
    absorbed = dot(kmg[...].reshape(1024, NOPE), qnp[...], ((1,), (1,)))
    own_head = (iota((1024, ROWS), 0) // 4) % 64 == iota((1024, ROWS), 1) // 8
    absorbed = jnp.where(own_head, absorbed, 0.0).astype(BF16)
    pick = ones_where(
        (iota((16, 1024), 1) // 256 == iota((16, 1024), 0) // 4) & (iota((16, 1024), 1) % 4 == iota((16, 1024), 0) % 4)
    )
    piece = dot(pick, absorbed).astype(BF16)
    qslots[c] = piece

    dz_copies = {
        o: go(remote(qslots.at[c], qslots.at[c], dz_send.at[o], dz_recv.at[o], at_z(o))) for o in (1, 7, 2, 6, 3, 5, 4)
    }
    dx_copies = []
    for k, i in enumerate((0, 1, 7, 2, 6, 3, 5, 4)):
        if i:
            dz_copies[i].wait_recv()
        slot = x * NZ + (z - i + NZ) % NZ
        for o in (2, 1, 3):
            n = k * 3 + o - 1
            dx_copies.append(go(remote(qslots.at[slot], qslots.at[slot], dx_send.at[n], dx_recv.at[n], at_x(o))))

    for copy in vb_copies:
        copy.wait_recv()
    vc_copies = [
        go(remote(v3.at[r], v3.at[r], v_send.at[10 + o], v_recv.at[10 + o], at_y(o))) for o in range(1, NY)
    ]
    take_apart(24, 64)

    copies[5].wait()
    row_of = iota((LAT, LAT), 0)
    line_up = ones_where(((row_of // 4) % 4) * 128 + (row_of // 16) * 4 + row_of % 4 == iota((LAT, LAT), 1))
    for copy in dx_copies:
        copy.wait_recv()
    q[:, 0:LAT] = dot(qslots[...].reshape(LAT, ROWS), line_up, ((0,), (0,))).astype(BF16)
    f1_copies = []
    for i in range(NX):
        o = (2, 1, 3, 0)[i]
        g = (x + o) % NX
        rows = pl.ds(pl.multiple_of(g * GROUP, GROUP), GROUP)
        q_rows = q[rows, :]
        top = None
        for k in range(KEYS // 512):
            cols = slice(k * 512, (k + 1) * 512)
            part = dot(q_rows, kt[:, cols])
            scores[:, cols] = part
            here = jnp.maximum(
                jnp.maximum(part[:, 0:128], part[:, 128:256]), jnp.maximum(part[:, 256:384], part[:, 384:512])
            )
            top = here if top is None else jnp.maximum(top, here)
        top = jnp.max(top, axis=1, keepdims=True)
        total = jnp.zeros((GROUP, 128), F32)
        weighted = jnp.zeros((GROUP, LAT), F32)
        for k in range(KEYS // 512):
            cols = slice(k * 512, (k + 1) * 512)
            e = jnp.exp2((scores[:, cols] - top) * SCALE2)
            total += e[:, 0:128] + e[:, 128:256] + e[:, 256:384] + e[:, 384:512]
            weighted += dot(e.astype(BF16), keys[cols, :])
        total = jnp.sum(total, axis=1, keepdims=True)
        if i < NX - 1:
            fs[i, :, 0:LAT] = weighted.astype(BF16)
            fs[i, :, LAT:WIDE] = pack_stats(top, total)
            f1_copies.append(go(remote(fs.at[i], f1.at[x], f1_send.at[o], f1_recv.at[o], at_x(o))))
        else:
            f1[x, :, 0:LAT] = weighted.astype(BF16)
            f1[x, :, LAT:WIDE] = pack_stats(top, total)

    for copy in f1_copies:
        copy.wait_recv()
    f2_copies = []
    for o in (4, 3, 5, 2, 6, 1, 7, 0):
        there = (z + o) % NZ
        rows = pl.ds(pl.multiple_of(there * 16, 16), 16)
        stats = [read_stats(f1[k, rows, LAT:WIDE]) for k in range(NX)]
        top = functools.reduce(jnp.maximum, [s[0] for s in stats])
        factors = [jnp.exp2((s[0] - top) * SCALE2) for s in stats]
        total = sum(f * s[1] for f, s in zip(factors, stats))
        weighted = sum(f * f1[k, rows, 0:LAT].astype(F32) for k, f in enumerate(factors))
        place = f2s if o else f2
        place[there, :, 0:LAT] = weighted.astype(BF16)
        place[there, :, LAT:WIDE] = pack_stats(top, total)
        if o:
            f2_copies.append(go(remote(f2s.at[there], f2.at[z], f2_send.at[o], f2_recv.at[o], at_z(o))))

    for i in (7, 8, 9, 10, 12):
        copies[i].wait()
    place = ones_where(iota((128, 8), 0) == iota((128, 8), 1))
    kr[512:640, :] = (dot(place[:, 0:4], nl[0]) + dot(place[:, 4:8], nl[1])).astype(BF16)
    new_rot = dot(place, nr[...]).astype(BF16)
    own = pl.ds(pl.multiple_of(c * 16, 16), 16)
    q_lat, q_rot = q[own, 0:LAT], q[own, LAT : LAT + ROPE]
    rot_scores = [dot(q_rot, sr[s]) for s in range(4)] + [dot(q_rot, new_rot, ((1,), (1,)))]
    recent = dot(q_lat, kr[...], ((1,), (1,))) + jnp.concatenate(rot_scores, axis=1)
    row, col = iota((16, WIDE), 0), iota((16, WIDE), 1)
    limit = jnp.zeros((16, WIDE), jnp.int32)
    for s in range(4):
        limit = jnp.where(col // 128 == s, suffix_length_ref[0, s], limit)
    suffix_valid = (col < 512) & (col // 128 == row % 4) & (col % 128 < limit)
    fresh = col - 512
    new_valid = (fresh >= 0) & (fresh < 8) & (fresh % 4 == row % 4) & (fresh // 4 <= (row // 4) % 2)
    valid = suffix_valid | new_valid
    recent = jnp.where(valid, recent, masked_score)
    recent_top = jnp.max(recent, axis=1, keepdims=True)
    e = jnp.where(valid, jnp.exp2((recent - recent_top) * SCALE2), 0.0)
    recent_total = jnp.sum(e, axis=1, keepdims=True)
    recent_sum = dot(e.astype(BF16), kr[...])

    for copy in vc_copies:
        copy.wait_recv()
    flat = v3[...].reshape(1024, VDIM)
    for k in range(2):
        latent = iota((LAT, 1024), 0)
        pick = ones_where(iota((LAT, 1024), 1) == (latent // 4) * 8 + k * 4 + latent % 4)
        vde[:, k * 128 : (k + 1) * 128] = dot(pick, flat).astype(BF16)

    for copy in f2_copies:
        copy.wait_recv()
    stats = [read_stats(f2[k, :, LAT:WIDE]) for k in range(NZ)]
    top = functools.reduce(jnp.maximum, [s[0] for s in stats] + [recent_top])
    factors = [jnp.exp2((s[0] - top) * SCALE2) for s in stats]
    recent_factor = jnp.exp2((recent_top - top) * SCALE2)
    total = sum(f * s[1] for f, s in zip(factors, stats)) + recent_factor * recent_total
    weighted = sum(f * f2[k, :, 0:LAT].astype(F32) for k, f in enumerate(factors)) + recent_factor * recent_sum
    latent_out = (weighted / total).astype(BF16)

    head_out = dot(latent_out, vde[...])
    head_out = jnp.concatenate([head_out[0:8, 0:128], head_out[8:16, 128:256]], axis=1).astype(BF16)
    hx_copies = []
    for o, away in ((2, 1), (2, 0), (1, 1), (1, 0), (3, 1), (3, 0), (0, 1), (0, 0)):
        there, core = (x + o) % NX, (t + away) % 2
        for k in range(0, NZ, 2):
            first = (there * NZ + k) * 2 + core
            part = [dot(head_out, outs[first + 2 * m], ((1,), (1,))) for m in range(2)]
            place = yb if o or away else yx
            place[there, core, k * 8 : k * 8 + 16] = jnp.concatenate(part, axis=0).astype(BF16)
        if o or away:
            n = o * 2 + away
            hx_copies.append(go(remote(yb.at[there, core], yx.at[x, t], h_send.at[n], h_recv.at[n], at_x(o, core))))
    for copy in hx_copies:
        copy.wait_recv()
    own_sum = sum(yx[k, core].astype(F32) for k in range(NX) for core in range(2))
    yzs[...] = own_sum.reshape(NZ, 8, 128)
    yz[z] = yzs[z]
    hz_copies = [
        go(remote(yzs.at[(z + o) % NZ], yz.at[z], h_send.at[7 + o], h_recv.at[7 + o], at_z(o)))
        for o in (4, 3, 5, 2, 6, 1, 7)
    ]
    for copy in hz_copies:
        copy.wait_recv()
    out_ref[...] = jnp.sum(yz[...], axis=0)

    for copy in sends:
        copy.wait_send()


def shards(
    query_nope,
    query_rope,
    key_map,
    value_map,
    out_map,
    prompt_latent,
    prompt_rope,
    prompt_lengths,
    suffix_latent,
    suffix_rope,
    suffix_lengths,
    new_latent,
    new_rope,
):
    any_spec = pl.BlockSpec(memory_space=pl.ANY)
    dma = pltpu.SemaphoreType.DMA
    vmem = pltpu.VMEM
    summed = pl.pallas_call(
        kernel,
        out_shape=jax.ShapeDtypeStruct((8, 128), F32),
        in_specs=[pl.BlockSpec(memory_space=pltpu.HBM)] * 2 + [any_spec] * 11,
        out_specs=pl.BlockSpec(memory_space=pltpu.VMEM),
        scratch_shapes=[
            vmem((ROWS, NOPE), BF16),
            vmem((ROWS, ROPE), BF16),
            vmem((ROWS, NOPE), BF16),
            vmem((NY, 256, NOPE), BF16),
            vmem((NX * NZ, 16, ROWS), BF16),
            vmem((ROWS, WIDE), BF16),
            vmem((KEYS, LAT), BF16),
            vmem((WIDE, KEYS), BF16),
            vmem((64, 224, VDIM), BF16),
            vmem((64, 128, 256), BF16),
            vmem((NX, NZ, 8, VDIM), BF16),
            vmem((NY, NX, NZ, 8, VDIM), BF16),
            vmem((LAT, 256), BF16),
            vmem((WIDE, LAT), BF16),
            vmem((4, ROPE, 128), BF16),
            vmem((2, 4, LAT), BF16),
            vmem((8, ROPE), BF16),
            vmem((GROUP, KEYS), F32),
            vmem((3, GROUP, WIDE), BF16),
            vmem((NX, GROUP, WIDE), BF16),
            vmem((NZ, 16, WIDE), BF16),
            vmem((NZ, 16, WIDE), BF16),
            vmem((NX, 2, NZ * 8, 128), BF16),
            vmem((NX, 2, NZ * 8, 128), BF16),
            vmem((NZ, 8, 128), F32),
            vmem((NZ, 8, 128), F32),
            pltpu.SMEM((1,), jnp.int32),
            pltpu.SMEM((1, 4), jnp.int32),
            dma((13,)),
            dma((NY,)),
            dma((NY,)),
            dma((14,)),
            dma((14,)),
            dma((NZ,)),
            dma((NZ,)),
            dma((24,)),
            dma((24,)),
            dma((NX,)),
            dma((NX,)),
            dma((NZ,)),
            dma((NZ,)),
            dma((15,)),
            dma((15,)),
        ],
        compiler_params=pltpu.CompilerParams(
            collective_id=0, has_side_effects=True, vmem_limit_bytes=56 * 1024 * 1024
        ),
        name="latent_attention",
    )(
        prompt_lengths,
        suffix_lengths,
        query_nope.reshape(ROWS, NOPE),
        query_rope.reshape(ROWS, ROPE),
        key_map.reshape(256, NOPE),
        value_map.reshape(NX, NZ, 8, VDIM),
        out_map.reshape(64, 224, VDIM),
        prompt_latent[0],
        prompt_rope[0],
        suffix_latent.reshape(512, LAT),
        suffix_rope[0],
        new_latent[0],
        new_rope.reshape(8, ROPE),
    )
    return summed[:, :FEATS].T.astype(BF16).reshape(1, FEATS, 2, 4)


def solution(mesh):
    placed = (
        P("replica", None, None, "tensor", None),
        P("replica", None, None, "tensor", None),
        P("tensor", ("replica", "context"), None),
        P("tensor", ("replica", "context"), None),
        P(None, "tensor", "context", None),
        P("replica", "context", None),
        P("replica", None, "context"),
        P("replica"),
        P("replica", None, None, None),
        P("replica", None, None, None),
        P("replica", None),
        P("replica", None, None, None),
        P("replica", None, None, None),
    )
    return jax.shard_map(
        shards,
        mesh=mesh,
        in_specs=placed,
        out_specs=P("replica", ("context", "tensor"), None, None),
        check_vma=False,
    )
```

```python
import functools
import math

import jax
import jax.numpy as jnp
from jax import lax
from jax.experimental import pallas as pl
from jax.experimental.pallas import tpu as pltpu
from jax.sharding import PartitionSpec as P

MESH = pl.DeviceIdType.MESH
F32 = jnp.float32
BF16 = jnp.bfloat16
masked_score = -1e30

NY, NX, NZ = 4, 4, 8
LAT, NOPE, ROPE, VDIM = 512, 128, 64, 128
KEYS = 4096
ROWS = 512
GROUP = 128
WIDE = 640
FEATS = 112
SCALE2 = (NOPE + ROPE) ** -0.5 * math.log2(math.e)


def iota(shape, axis):
    return lax.broadcasted_iota(jnp.int32, shape, axis)


def dot(a, b, dims=((1,), (0,))):
    return lax.dot_general(a, b, (dims, ((), ())), preferred_element_type=F32)


def ones_where(mask):
    return jnp.where(mask, 1.0, 0.0).astype(BF16)


def split3(x):
    first = x.astype(BF16).astype(F32)
    second = (x - first).astype(BF16).astype(F32)
    return first, second, x - first - second


def pack_stats(top, total):
    lanes = iota((top.shape[0], 128), 1)
    packed = jnp.zeros((top.shape[0], 128), F32)
    for k, part in enumerate(split3(top) + split3(total)):
        packed = jnp.where(lanes == k, part, packed)
    return packed.astype(BF16)


def read_stats(packed):
    wide = packed.astype(F32)
    top = wide[:, 0:1] + wide[:, 1:2] + wide[:, 2:3]
    total = wide[:, 3:4] + wide[:, 4:5] + wide[:, 5:6]
    return top, total


def kernel(
    length_hbm,
    suffix_length_hbm,
    qn_hbm,
    qr_hbm,
    km_hbm,
    vm_hbm,
    om_hbm,
    keys_hbm,
    rope_hbm,
    sl_hbm,
    sr_hbm,
    nl_hbm,
    nr_hbm,
    out_ref,
    qn,
    qr,
    qnp,
    kmg,
    qslots,
    q,
    keys,
    kt,
    om,
    outs,
    v1,
    v3,
    vde,
    kr,
    sr,
    nl,
    nr,
    scores,
    fs,
    f1,
    f2s,
    f2,
    yb,
    yx,
    yz,
    yzs,
    length_ref,
    suffix_length_ref,
    load_sem,
    b_send,
    b_recv,
    v_send,
    v_recv,
    dz_send,
    dz_recv,
    dx_send,
    dx_recv,
    f1_send,
    f1_recv,
    f2_send,
    f2_recv,
    h_send,
    h_recv,
):
    r = lax.axis_index("replica")
    c = lax.axis_index("context")
    t = lax.axis_index("tensor")
    x, z = c // NZ, c % NZ

    def at_y(o):
        return ((r + o) % NY, c, t)

    def at_x(o, core=t):
        return (r, ((x + o) % NX) * NZ + z, core)

    def at_z(o):
        return (r, x * NZ + (z + o) % NZ, t)

    def remote(src, dst, send, recv, device):
        return pltpu.make_async_remote_copy(
            src_ref=src, dst_ref=dst, send_sem=send, recv_sem=recv, device_id=device, device_id_type=MESH
        )

    loads = [
        (qn_hbm, qn),
        (qr_hbm, qr),
        (keys_hbm, keys),
        (om_hbm, om),
        (km_hbm, kmg.at[r]),
        (rope_hbm, kt.at[pl.ds(LAT, ROPE)]),
        (vm_hbm.at[x], v1.at[x]),
        (sl_hbm, kr.at[pl.ds(0, 512)]),
        (sr_hbm, sr),
        (nl_hbm, nl),
        (nr_hbm, nr),
        (length_hbm, length_ref),
        (suffix_length_hbm, suffix_length_ref),
    ]
    copies = [pltpu.make_async_copy(a, b, load_sem.at[i]) for i, (a, b) in enumerate(loads)]
    barrier = pltpu.get_barrier_semaphore()
    peers = [at_y(o) for o in range(1, NY)] + [at_x(o) for o in range(1, NX)]
    peers += [at_x(o, 1 - t) for o in range(NX)] + [at_z(o) for o in range(1, NZ)]
    for peer in peers:
        pl.semaphore_signal(barrier, inc=1, device_id=peer, device_id_type=MESH)
    for i in (4, 6, 0, 1, 11, 2, 3, 5, 7, 8, 9, 10, 12):
        copies[i].start()

    pl.semaphore_wait(barrier, len(peers))

    sends = []

    def go(copy):
        copy.start()
        sends.append(copy)
        return copy

    copies[4].wait()
    b_copies = [go(remote(kmg.at[r], kmg.at[r], b_send.at[o], b_recv.at[o], at_y(o))) for o in range(1, NY)]
    va_copies = [
        go(remote(vm_hbm.at[(x + o) % NX], v1.at[x], v_send.at[o], v_recv.at[o], at_x(o))) for o in range(1, NX)
    ]

    copies[0].wait()
    copies[1].wait()
    order = ones_where(
        (iota((ROWS, ROWS), 0) // 8 == iota((ROWS, ROWS), 1) % 64)
        & (iota((ROWS, ROWS), 0) % 8 == iota((ROWS, ROWS), 1) // 64)
    )
    qnp[...] = dot(order, qn[...]).astype(BF16)
    widen = ones_where(iota((ROPE, 128), 0) == iota((ROPE, 128), 1))
    rope_rows = dot(order, dot(qr[...], widen).astype(BF16))
    q[:, LAT:WIDE] = jnp.where(iota((ROWS, 128), 1) == ROPE, 1.0, rope_rows).astype(BF16)

    copies[11].wait()
    position = c * KEYS + iota((64, KEYS), 1)
    beyond = (position >= length_ref[0]) & (iota((64, KEYS), 0) == 0)
    kt[LAT + ROPE : WIDE, :] = jnp.where(beyond, masked_score, 0.0).astype(BF16)
    copies[2].wait()

    @pl.loop(0, KEYS // 512)
    def _(i):
        rows = pl.ds(pl.multiple_of(i * 512, 512), 512)
        kt[0:LAT, rows] = keys[rows, :].T

    copies[6].wait()
    for copy in va_copies:
        copy.wait_recv()
    v3[r, :, z] = v1[:, z]
    vb_copies = [
        go(remote(v1.at[:, (z + o) % NZ], v3.at[r, :, z], v_send.at[3 + o], v_recv.at[3 + o], at_z(o)))
        for o in range(1, NZ)
    ]

    copies[3].wait()
    apart = ones_where(iota((256, 224), 1) == (iota((256, 224), 0) % 128) * 2 + iota((256, 224), 0) // 128)
    apart = jnp.where(iota((256, 224), 0) % 128 < FEATS, apart, jnp.zeros_like(apart))

    def take_apart(begin, end):
        @pl.loop(begin, end, step=8)
        def _(first):
            for d in range(8):
                both = dot(apart, om[first + d]).astype(BF16)
                outs[first + d, :, 0:128] = both[0:128]
                outs[first + d, :, 128:256] = both[128:256]

    take_apart(0, 24)

    for copy in b_copies:
        copy.wait_recv()
    absorbed = dot(kmg[...].reshape(1024, NOPE), qnp[...], ((1,), (1,)))
    own_head = (iota((1024, ROWS), 0) // 4) % 64 == iota((1024, ROWS), 1) // 8
    absorbed = jnp.where(own_head, absorbed, 0.0).astype(BF16)
    pick = ones_where(
        (iota((16, 1024), 1) // 256 == iota((16, 1024), 0) // 4) & (iota((16, 1024), 1) % 4 == iota((16, 1024), 0) % 4)
    )
    piece = dot(pick, absorbed).astype(BF16)
    qslots[c] = piece

    dz_copies = {
        o: go(remote(qslots.at[c], qslots.at[c], dz_send.at[o], dz_recv.at[o], at_z(o))) for o in (1, 7, 2, 6, 3, 5, 4)
    }
    dx_copies = []
    for k, i in enumerate((0, 1, 7, 2, 6, 3, 5, 4)):
        if i:
            dz_copies[i].wait_recv()
        slot = x * NZ + (z - i + NZ) % NZ
        for o in (2, 1, 3):
            n = k * 3 + o - 1
            dx_copies.append(go(remote(qslots.at[slot], qslots.at[slot], dx_send.at[n], dx_recv.at[n], at_x(o))))

    for copy in vb_copies:
        copy.wait_recv()
    vc_copies = [
        go(remote(v3.at[r], v3.at[r], v_send.at[10 + o], v_recv.at[10 + o], at_y(o))) for o in range(1, NY)
    ]
    take_apart(24, 64)

    copies[5].wait()
    row_of = iota((LAT, LAT), 0)
    line_up = ones_where(((row_of // 4) % 4) * 128 + (row_of // 16) * 4 + row_of % 4 == iota((LAT, LAT), 1))
    for copy in dx_copies:
        copy.wait_recv()
    q[:, 0:LAT] = dot(qslots[...].reshape(LAT, ROWS), line_up, ((0,), (0,))).astype(BF16)
    f1_copies = []
    for i in range(NX):
        o = (2, 1, 3, 0)[i]
        g = (x + o) % NX
        rows = pl.ds(pl.multiple_of(g * GROUP, GROUP), GROUP)
        q_rows = q[rows, :]
        top = None
        for k in range(KEYS // 512):
            cols = slice(k * 512, (k + 1) * 512)
            part = dot(q_rows, kt[:, cols])
            scores[:, cols] = part
            here = jnp.maximum(
                jnp.maximum(part[:, 0:128], part[:, 128:256]), jnp.maximum(part[:, 256:384], part[:, 384:512])
            )
            top = here if top is None else jnp.maximum(top, here)
        top = jnp.max(top, axis=1, keepdims=True)
        total = jnp.zeros((GROUP, 128), F32)
        weighted = jnp.zeros((GROUP, LAT), F32)
        for k in range(KEYS // 512):
            cols = slice(k * 512, (k + 1) * 512)
            e = jnp.exp2((scores[:, cols] - top) * SCALE2)
            total += e[:, 0:128] + e[:, 128:256] + e[:, 256:384] + e[:, 384:512]
            weighted += dot(e.astype(BF16), keys[cols, :])
        total = jnp.sum(total, axis=1, keepdims=True)
        if i < NX - 1:
            fs[i, :, 0:LAT] = weighted.astype(BF16)
            fs[i, :, LAT:WIDE] = pack_stats(top, total)
            f1_copies.append(go(remote(fs.at[i], f1.at[x], f1_send.at[o], f1_recv.at[o], at_x(o))))
        else:
            f1[x, :, 0:LAT] = weighted.astype(BF16)
            f1[x, :, LAT:WIDE] = pack_stats(top, total)

    for copy in f1_copies:
        copy.wait_recv()
    f2_copies = []
    for o in (4, 3, 5, 2, 6, 1, 7, 0):
        there = (z + o) % NZ
        rows = pl.ds(pl.multiple_of(there * 16, 16), 16)
        stats = [read_stats(f1[k, rows, LAT:WIDE]) for k in range(NX)]
        top = functools.reduce(jnp.maximum, [s[0] for s in stats])
        factors = [jnp.exp2((s[0] - top) * SCALE2) for s in stats]
        total = sum(f * s[1] for f, s in zip(factors, stats))
        weighted = sum(f * f1[k, rows, 0:LAT].astype(F32) for k, f in enumerate(factors))
        place = f2s if o else f2
        place[there, :, 0:LAT] = weighted.astype(BF16)
        place[there, :, LAT:WIDE] = pack_stats(top, total)
        if o:
            f2_copies.append(go(remote(f2s.at[there], f2.at[z], f2_send.at[o], f2_recv.at[o], at_z(o))))

    early_sends = sends[: -(NZ - 1)]

    for i in (7, 8, 9, 10, 12):
        copies[i].wait()
    place = ones_where(iota((128, 8), 0) == iota((128, 8), 1))
    kr[512:640, :] = (dot(place[:, 0:4], nl[0]) + dot(place[:, 4:8], nl[1])).astype(BF16)
    new_rot = dot(place, nr[...]).astype(BF16)
    own = pl.ds(pl.multiple_of(c * 16, 16), 16)
    q_lat, q_rot = q[own, 0:LAT], q[own, LAT : LAT + ROPE]
    rot_scores = [dot(q_rot, sr[s]) for s in range(4)] + [dot(q_rot, new_rot, ((1,), (1,)))]
    recent = dot(q_lat, kr[...], ((1,), (1,))) + jnp.concatenate(rot_scores, axis=1)
    row, col = iota((16, WIDE), 0), iota((16, WIDE), 1)
    limit = jnp.zeros((16, WIDE), jnp.int32)
    for s in range(4):
        limit = jnp.where(col // 128 == s, suffix_length_ref[0, s], limit)
    suffix_valid = (col < 512) & (col // 128 == row % 4) & (col % 128 < limit)
    fresh = col - 512
    new_valid = (fresh >= 0) & (fresh < 8) & (fresh % 4 == row % 4) & (fresh // 4 <= (row // 4) % 2)
    valid = suffix_valid | new_valid
    recent = jnp.where(valid, recent, masked_score)
    recent_top = jnp.max(recent, axis=1, keepdims=True)
    e = jnp.where(valid, jnp.exp2((recent - recent_top) * SCALE2), 0.0)
    recent_total = jnp.sum(e, axis=1, keepdims=True)
    recent_sum = dot(e.astype(BF16), kr[...])

    for copy in vc_copies:
        copy.wait_recv()
    flat = v3[...].reshape(1024, VDIM)
    for k in range(2):
        latent = iota((LAT, 1024), 0)
        pick = ones_where(iota((LAT, 1024), 1) == (latent // 4) * 8 + k * 4 + latent % 4)
        vde[:, k * 128 : (k + 1) * 128] = dot(pick, flat).astype(BF16)

    for copy in early_sends:
        copy.wait_send()

    for copy in f2_copies:
        copy.wait_recv()
    stats = [read_stats(f2[k, :, LAT:WIDE]) for k in range(NZ)]
    top = functools.reduce(jnp.maximum, [s[0] for s in stats] + [recent_top])
    factors = [jnp.exp2((s[0] - top) * SCALE2) for s in stats]
    recent_factor = jnp.exp2((recent_top - top) * SCALE2)
    total = sum(f * s[1] for f, s in zip(factors, stats)) + recent_factor * recent_total
    weighted = sum(f * f2[k, :, 0:LAT].astype(F32) for k, f in enumerate(factors)) + recent_factor * recent_sum
    latent_out = (weighted / total).astype(BF16)

    head_out = dot(latent_out, vde[...])
    head_out = jnp.concatenate([head_out[0:8, 0:128], head_out[8:16, 128:256]], axis=1).astype(BF16)
    hx_copies = []
    for o, away in ((2, 1), (2, 0), (1, 1), (1, 0), (3, 1), (3, 0), (0, 1), (0, 0)):
        there, core = (x + o) % NX, (t + away) % 2
        for k in range(0, NZ, 2):
            first = (there * NZ + k) * 2 + core
            part = [dot(head_out, outs[first + 2 * m], ((1,), (1,))) for m in range(2)]
            place = yb if o or away else yx
            place[there, core, k * 8 : k * 8 + 16] = jnp.concatenate(part, axis=0).astype(BF16)
        if o or away:
            n = o * 2 + away
            hx_copies.append(go(remote(yb.at[there, core], yx.at[x, t], h_send.at[n], h_recv.at[n], at_x(o, core))))
    for copy in hx_copies:
        copy.wait_recv()
    own_sum = sum(yx[k, core].astype(F32) for k in range(NX) for core in range(2))
    yzs[...] = own_sum.reshape(NZ, 8, 128)
    yz[z] = yzs[z]
    hz_copies = [
        go(remote(yzs.at[(z + o) % NZ], yz.at[z], h_send.at[7 + o], h_recv.at[7 + o], at_z(o)))
        for o in (4, 3, 5, 2, 6, 1, 7)
    ]
    for copy in hz_copies:
        copy.wait_recv()
    out_ref[...] = jnp.sum(yz[...], axis=0)

    for copy in sends[len(early_sends) :]:
        copy.wait_send()


def shards(
    query_nope,
    query_rope,
    key_map,
    value_map,
    out_map,
    prompt_latent,
    prompt_rope,
    prompt_lengths,
    suffix_latent,
    suffix_rope,
    suffix_lengths,
    new_latent,
    new_rope,
):
    any_spec = pl.BlockSpec(memory_space=pl.ANY)
    dma = pltpu.SemaphoreType.DMA
    vmem = pltpu.VMEM
    summed = pl.pallas_call(
        kernel,
        out_shape=jax.ShapeDtypeStruct((8, 128), F32),
        in_specs=[pl.BlockSpec(memory_space=pltpu.HBM)] * 2 + [any_spec] * 11,
        out_specs=pl.BlockSpec(memory_space=pltpu.VMEM),
        scratch_shapes=[
            vmem((ROWS, NOPE), BF16),
            vmem((ROWS, ROPE), BF16),
            vmem((ROWS, NOPE), BF16),
            vmem((NY, 256, NOPE), BF16),
            vmem((NX * NZ, 16, ROWS), BF16),
            vmem((ROWS, WIDE), BF16),
            vmem((KEYS, LAT), BF16),
            vmem((WIDE, KEYS), BF16),
            vmem((64, 224, VDIM), BF16),
            vmem((64, 128, 256), BF16),
            vmem((NX, NZ, 8, VDIM), BF16),
            vmem((NY, NX, NZ, 8, VDIM), BF16),
            vmem((LAT, 256), BF16),
            vmem((WIDE, LAT), BF16),
            vmem((4, ROPE, 128), BF16),
            vmem((2, 4, LAT), BF16),
            vmem((8, ROPE), BF16),
            vmem((GROUP, KEYS), F32),
            vmem((3, GROUP, WIDE), BF16),
            vmem((NX, GROUP, WIDE), BF16),
            vmem((NZ, 16, WIDE), BF16),
            vmem((NZ, 16, WIDE), BF16),
            vmem((NX, 2, NZ * 8, 128), BF16),
            vmem((NX, 2, NZ * 8, 128), BF16),
            vmem((NZ, 8, 128), F32),
            vmem((NZ, 8, 128), F32),
            pltpu.SMEM((1,), jnp.int32),
            pltpu.SMEM((1, 4), jnp.int32),
            dma((13,)),
            dma((NY,)),
            dma((NY,)),
            dma((14,)),
            dma((14,)),
            dma((NZ,)),
            dma((NZ,)),
            dma((24,)),
            dma((24,)),
            dma((NX,)),
            dma((NX,)),
            dma((NZ,)),
            dma((NZ,)),
            dma((15,)),
            dma((15,)),
        ],
        compiler_params=pltpu.CompilerParams(
            collective_id=0, has_side_effects=True, vmem_limit_bytes=56 * 1024 * 1024
        ),
        name="latent_attention",
    )(
        prompt_lengths,
        suffix_lengths,
        query_nope.reshape(ROWS, NOPE),
        query_rope.reshape(ROWS, ROPE),
        key_map.reshape(256, NOPE),
        value_map.reshape(NX, NZ, 8, VDIM),
        out_map.reshape(64, 224, VDIM),
        prompt_latent[0],
        prompt_rope[0],
        suffix_latent.reshape(512, LAT),
        suffix_rope[0],
        new_latent[0],
        new_rope.reshape(8, ROPE),
    )
    return summed[:, :FEATS].T.astype(BF16).reshape(1, FEATS, 2, 4)


def solution(mesh):
    placed = (
        P("replica", None, None, "tensor", None),
        P("replica", None, None, "tensor", None),
        P("tensor", ("replica", "context"), None),
        P("tensor", ("replica", "context"), None),
        P(None, "tensor", "context", None),
        P("replica", "context", None),
        P("replica", None, "context"),
        P("replica"),
        P("replica", None, None, None),
        P("replica", None, None, None),
        P("replica", None),
        P("replica", None, None, None),
        P("replica", None, None, None),
    )
    return jax.shard_map(
        shards,
        mesh=mesh,
        in_specs=placed,
        out_specs=P("replica", ("context", "tensor"), None, None),
        check_vma=False,
    )
```

```python
import functools
import math

import jax
import jax.numpy as jnp
from jax import lax
from jax.experimental import pallas as pl
from jax.experimental.pallas import tpu as pltpu
from jax.sharding import PartitionSpec as P

MESH = pl.DeviceIdType.MESH
F32 = jnp.float32
BF16 = jnp.bfloat16
masked_score = -1e30

NY, NX, NZ = 4, 4, 8
LAT, NOPE, ROPE, VDIM = 512, 128, 64, 128
KEYS = 4096
ROWS = 512
GROUP = 128
WIDE = 640
FEATS = 112
SCALE2 = (NOPE + ROPE) ** -0.5 * math.log2(math.e)


def iota(shape, axis):
    return lax.broadcasted_iota(jnp.int32, shape, axis)


def dot(a, b, dims=((1,), (0,))):
    return lax.dot_general(a, b, (dims, ((), ())), preferred_element_type=F32)


def ones_where(mask):
    return jnp.where(mask, 1.0, 0.0).astype(BF16)


def split3(x):
    first = x.astype(BF16).astype(F32)
    second = (x - first).astype(BF16).astype(F32)
    return first, second, x - first - second


def pack_stats(top, total):
    lanes = iota((top.shape[0], 128), 1)
    packed = jnp.zeros((top.shape[0], 128), F32)
    for k, part in enumerate(split3(top) + split3(total)):
        packed = jnp.where(lanes == k, part, packed)
    return packed.astype(BF16)


def read_stats(packed):
    wide = packed.astype(F32)
    top = wide[:, 0:1] + wide[:, 1:2] + wide[:, 2:3]
    total = wide[:, 3:4] + wide[:, 4:5] + wide[:, 5:6]
    return top, total


def kernel(
    length_hbm,
    suffix_length_hbm,
    qn_hbm,
    qr_hbm,
    km_hbm,
    vm_hbm,
    om_hbm,
    keys_hbm,
    rope_hbm,
    sl_hbm,
    sr_hbm,
    nl_hbm,
    nr_hbm,
    out_ref,
    qn,
    qr,
    qnp,
    own_head,
    kmg,
    qslots,
    q,
    keys,
    kt,
    om,
    outs,
    v1,
    v3,
    vde,
    kr,
    sr,
    nl,
    nr,
    scores,
    fs,
    f1,
    f2s,
    f2,
    yb,
    yx,
    yz,
    yzs,
    length_ref,
    suffix_length_ref,
    load_sem,
    b_send,
    b_recv,
    v_send,
    v_recv,
    dz_send,
    dz_recv,
    dx_send,
    dx_recv,
    f1_send,
    f1_recv,
    f2_send,
    f2_recv,
    h_send,
    h_recv,
):
    r = lax.axis_index("replica")
    c = lax.axis_index("context")
    t = lax.axis_index("tensor")
    x, z = c // NZ, c % NZ

    def at_y(o):
        return ((r + o) % NY, c, t)

    def at_x(o, core=t):
        return (r, ((x + o) % NX) * NZ + z, core)

    def at_z(o):
        return (r, x * NZ + (z + o) % NZ, t)

    def remote(src, dst, send, recv, device):
        return pltpu.make_async_remote_copy(
            src_ref=src, dst_ref=dst, send_sem=send, recv_sem=recv, device_id=device, device_id_type=MESH
        )

    loads = [
        (qn_hbm, qn),
        (qr_hbm, qr),
        (keys_hbm, keys),
        (om_hbm, om),
        (km_hbm, kmg.at[r]),
        (rope_hbm, kt.at[pl.ds(LAT, ROPE)]),
        (vm_hbm.at[x], v1.at[x]),
        (sl_hbm, kr.at[pl.ds(0, 512)]),
        (sr_hbm, sr),
        (nl_hbm, nl),
        (nr_hbm, nr),
        (length_hbm, length_ref),
        (suffix_length_hbm, suffix_length_ref),
    ]
    copies = [pltpu.make_async_copy(a, b, load_sem.at[i]) for i, (a, b) in enumerate(loads)]
    barrier = pltpu.get_barrier_semaphore()
    peers = [at_y(o) for o in range(1, NY)] + [at_x(o) for o in range(1, NX)]
    peers += [at_x(o, 1 - t) for o in range(NX)] + [at_z(o) for o in range(1, NZ)]
    for peer in peers:
        pl.semaphore_signal(barrier, inc=1, device_id=peer, device_id_type=MESH)
    for i in (4, 6, 0, 1, 11, 2, 3, 5, 7, 8, 9, 10, 12):
        copies[i].start()

    pl.semaphore_wait(barrier, len(peers))

    sends = []

    def go(copy):
        copy.start()
        sends.append(copy)
        return copy

    copies[4].wait()
    b_copies = [go(remote(kmg.at[r], kmg.at[r], b_send.at[o], b_recv.at[o], at_y(o))) for o in range(1, NY)]
    va_copies = [
        go(remote(vm_hbm.at[(x + o) % NX], v1.at[x], v_send.at[o], v_recv.at[o], at_x(o))) for o in range(1, NX)
    ]

    copies[0].wait()
    copies[1].wait()
    order = ones_where(
        (iota((ROWS, ROWS), 0) // 8 == iota((ROWS, ROWS), 1) % 64)
        & (iota((ROWS, ROWS), 0) % 8 == iota((ROWS, ROWS), 1) // 64)
    )
    qnp[...] = dot(order, qn[...]).astype(BF16)
    widen = ones_where(iota((ROPE, 128), 0) == iota((ROPE, 128), 1))
    rope_rows = dot(order, dot(qr[...], widen).astype(BF16))
    q[:, LAT:WIDE] = jnp.where(iota((ROWS, 128), 1) == ROPE, 1.0, rope_rows).astype(BF16)

    copies[11].wait()
    position = c * KEYS + iota((64, KEYS), 1)
    beyond = (position >= length_ref[0]) & (iota((64, KEYS), 0) == 0)
    kt[LAT + ROPE : WIDE, :] = jnp.where(beyond, masked_score, 0.0).astype(BF16)
    copies[2].wait()

    @pl.loop(0, KEYS // 512)
    def _(i):
        rows = pl.ds(pl.multiple_of(i * 512, 512), 512)
        kt[0:LAT, rows] = keys[rows, :].T

    copies[6].wait()
    for copy in va_copies:
        copy.wait_recv()
    v3[r, :, z] = v1[:, z]
    vb_copies = [
        go(remote(v1.at[:, (z + o) % NZ], v3.at[r, :, z], v_send.at[3 + o], v_recv.at[3 + o], at_z(o)))
        for o in range(1, NZ)
    ]

    copies[3].wait()
    apart = ones_where(iota((256, 224), 1) == (iota((256, 224), 0) % 128) * 2 + iota((256, 224), 0) // 128)
    apart = jnp.where(iota((256, 224), 0) % 128 < FEATS, apart, jnp.zeros_like(apart))

    def take_apart(begin, end):
        @pl.loop(begin, end, step=8)
        def _(first):
            for d in range(8):
                both = dot(apart, om[first + d]).astype(BF16)
                outs[first + d, :, 0:128] = both[0:128]
                outs[first + d, :, 128:256] = both[128:256]

    take_apart(0, 24)

    own_head[...] = jnp.where(iota((256, ROWS), 0) // 4 == iota((256, ROWS), 1) // 8, 1.0, 0.0)

    for copy in b_copies:
        copy.wait_recv()
    absorbed = dot(kmg[...].reshape(1024, NOPE), qnp[...], ((1,), (1,)))
    absorbed = (absorbed.reshape(NY, 256, ROWS) * own_head[...]).astype(BF16).reshape(1024, ROWS)
    pick = ones_where(
        (iota((16, 1024), 1) // 256 == iota((16, 1024), 0) // 4) & (iota((16, 1024), 1) % 4 == iota((16, 1024), 0) % 4)
    )
    piece = dot(pick, absorbed).astype(BF16)
    qslots[c] = piece

    dz_copies = {
        o: go(remote(qslots.at[c], qslots.at[c], dz_send.at[o], dz_recv.at[o], at_z(o))) for o in (1, 7, 2, 6, 3, 5, 4)
    }
    dx_copies = []
    for k, i in enumerate((0, 1, 7, 2, 6, 3, 5, 4)):
        if i:
            dz_copies[i].wait_recv()
        slot = x * NZ + (z - i + NZ) % NZ
        for o in (2, 1, 3):
            n = k * 3 + o - 1
            dx_copies.append(go(remote(qslots.at[slot], qslots.at[slot], dx_send.at[n], dx_recv.at[n], at_x(o))))

    for copy in vb_copies:
        copy.wait_recv()
    vc_copies = [
        go(remote(v3.at[r], v3.at[r], v_send.at[10 + o], v_recv.at[10 + o], at_y(o))) for o in range(1, NY)
    ]
    take_apart(24, 64)

    copies[5].wait()
    row_of = iota((LAT, LAT), 0)
    line_up = ones_where(((row_of // 4) % 4) * 128 + (row_of // 16) * 4 + row_of % 4 == iota((LAT, LAT), 1))
    for copy in dx_copies:
        copy.wait_recv()
    f1_copies = []
    for i in range(NX):
        o = (2, 1, 3, 0)[i]
        g = (x + o) % NX
        rows = pl.ds(pl.multiple_of(g * GROUP, GROUP), GROUP)
        q[rows, 0:LAT] = dot(qslots[:, :, rows].reshape(LAT, GROUP), line_up, ((0,), (0,))).astype(BF16)
        q_rows = q[rows, :]
        top = None
        for k in range(KEYS // 512):
            cols = slice(k * 512, (k + 1) * 512)
            part = dot(q_rows, kt[:, cols])
            scores[:, cols] = part
            here = jnp.maximum(
                jnp.maximum(part[:, 0:128], part[:, 128:256]), jnp.maximum(part[:, 256:384], part[:, 384:512])
            )
            top = here if top is None else jnp.maximum(top, here)
        top = jnp.max(top, axis=1, keepdims=True)
        total = jnp.zeros((GROUP, 128), F32)
        weighted = jnp.zeros((GROUP, LAT), F32)
        for k in range(KEYS // 512):
            cols = slice(k * 512, (k + 1) * 512)
            e = jnp.exp2((scores[:, cols] - top) * SCALE2)
            total += e[:, 0:128] + e[:, 128:256] + e[:, 256:384] + e[:, 384:512]
            weighted += dot(e.astype(BF16), keys[cols, :])
        total = jnp.sum(total, axis=1, keepdims=True)
        if i < NX - 1:
            fs[i, :, 0:LAT] = weighted.astype(BF16)
            fs[i, :, LAT:WIDE] = pack_stats(top, total)
            f1_copies.append(go(remote(fs.at[i], f1.at[x], f1_send.at[o], f1_recv.at[o], at_x(o))))
        else:
            f1[x, :, 0:LAT] = weighted.astype(BF16)
            f1[x, :, LAT:WIDE] = pack_stats(top, total)

    for copy in f1_copies:
        copy.wait_recv()
    f2_copies = []
    for o in (4, 3, 5, 2, 6, 1, 7, 0):
        there = (z + o) % NZ
        rows = pl.ds(pl.multiple_of(there * 16, 16), 16)
        stats = [read_stats(f1[k, rows, LAT:WIDE]) for k in range(NX)]
        top = functools.reduce(jnp.maximum, [s[0] for s in stats])
        factors = [jnp.exp2((s[0] - top) * SCALE2) for s in stats]
        total = sum(f * s[1] for f, s in zip(factors, stats))
        weighted = sum(f * f1[k, rows, 0:LAT].astype(F32) for k, f in enumerate(factors))
        place = f2s if o else f2
        place[there, :, 0:LAT] = weighted.astype(BF16)
        place[there, :, LAT:WIDE] = pack_stats(top, total)
        if o:
            f2_copies.append(go(remote(f2s.at[there], f2.at[z], f2_send.at[o], f2_recv.at[o], at_z(o))))

    early_sends = sends[: -(NZ - 1)]

    for i in (7, 8, 9, 10, 12):
        copies[i].wait()
    place = ones_where(iota((128, 8), 0) == iota((128, 8), 1))
    kr[512:640, :] = (dot(place[:, 0:4], nl[0]) + dot(place[:, 4:8], nl[1])).astype(BF16)
    new_rot = dot(place, nr[...]).astype(BF16)
    own = pl.ds(pl.multiple_of(c * 16, 16), 16)
    q_lat, q_rot = q[own, 0:LAT], q[own, LAT : LAT + ROPE]
    rot_scores = [dot(q_rot, sr[s]) for s in range(4)] + [dot(q_rot, new_rot, ((1,), (1,)))]
    recent = dot(q_lat, kr[...], ((1,), (1,))) + jnp.concatenate(rot_scores, axis=1)
    row, col = iota((16, WIDE), 0), iota((16, WIDE), 1)
    limit = jnp.zeros((16, WIDE), jnp.int32)
    for s in range(4):
        limit = jnp.where(col // 128 == s, suffix_length_ref[0, s], limit)
    suffix_valid = (col < 512) & (col // 128 == row % 4) & (col % 128 < limit)
    fresh = col - 512
    new_valid = (fresh >= 0) & (fresh < 8) & (fresh % 4 == row % 4) & (fresh // 4 <= (row // 4) % 2)
    valid = suffix_valid | new_valid
    recent = jnp.where(valid, recent, masked_score)
    recent_top = jnp.max(recent, axis=1, keepdims=True)
    e = jnp.where(valid, jnp.exp2((recent - recent_top) * SCALE2), 0.0)
    recent_total = jnp.sum(e, axis=1, keepdims=True)
    recent_sum = dot(e.astype(BF16), kr[...])

    for copy in vc_copies:
        copy.wait_recv()
    flat = v3[...].reshape(1024, VDIM)
    for k in range(2):
        latent = iota((LAT, 1024), 0)
        pick = ones_where(iota((LAT, 1024), 1) == (latent // 4) * 8 + k * 4 + latent % 4)
        vde[:, k * 128 : (k + 1) * 128] = dot(pick, flat).astype(BF16)

    for copy in early_sends:
        copy.wait_send()

    for copy in f2_copies:
        copy.wait_recv()
    stats = [read_stats(f2[k, :, LAT:WIDE]) for k in range(NZ)]
    top = functools.reduce(jnp.maximum, [s[0] for s in stats] + [recent_top])
    factors = [jnp.exp2((s[0] - top) * SCALE2) for s in stats]
    recent_factor = jnp.exp2((recent_top - top) * SCALE2)
    total = sum(f * s[1] for f, s in zip(factors, stats)) + recent_factor * recent_total
    weighted = sum(f * f2[k, :, 0:LAT].astype(F32) for k, f in enumerate(factors)) + recent_factor * recent_sum
    latent_out = (weighted / total).astype(BF16)

    head_out = dot(latent_out, vde[...])
    head_out = jnp.concatenate([head_out[0:8, 0:128], head_out[8:16, 128:256]], axis=1).astype(BF16)
    hx_copies = []
    for o, away in ((2, 1), (2, 0), (1, 1), (1, 0), (3, 1), (3, 0), (0, 1), (0, 0)):
        there, core = (x + o) % NX, (t + away) % 2
        for k in range(0, NZ, 2):
            first = (there * NZ + k) * 2 + core
            part = [dot(head_out, outs[first + 2 * m], ((1,), (1,))) for m in range(2)]
            place = yb if o or away else yx
            place[there, core, k * 8 : k * 8 + 16] = jnp.concatenate(part, axis=0).astype(BF16)
        if o or away:
            n = o * 2 + away
            hx_copies.append(go(remote(yb.at[there, core], yx.at[x, t], h_send.at[n], h_recv.at[n], at_x(o, core))))
    for copy in hx_copies:
        copy.wait_recv()
    own_sum = sum(yx[k, core].astype(F32) for k in range(NX) for core in range(2))
    yzs[...] = own_sum.reshape(NZ, 8, 128)
    yz[z] = yzs[z]
    hz_copies = [
        go(remote(yzs.at[(z + o) % NZ], yz.at[z], h_send.at[7 + o], h_recv.at[7 + o], at_z(o)))
        for o in (4, 3, 5, 2, 6, 1, 7)
    ]
    for copy in hz_copies:
        copy.wait_recv()
    out_ref[...] = jnp.sum(yz[...], axis=0)

    for copy in sends[len(early_sends) :]:
        copy.wait_send()


def shards(
    query_nope,
    query_rope,
    key_map,
    value_map,
    out_map,
    prompt_latent,
    prompt_rope,
    prompt_lengths,
    suffix_latent,
    suffix_rope,
    suffix_lengths,
    new_latent,
    new_rope,
):
    any_spec = pl.BlockSpec(memory_space=pl.ANY)
    dma = pltpu.SemaphoreType.DMA
    vmem = pltpu.VMEM
    summed = pl.pallas_call(
        kernel,
        out_shape=jax.ShapeDtypeStruct((8, 128), F32),
        in_specs=[pl.BlockSpec(memory_space=pltpu.HBM)] * 2 + [any_spec] * 11,
        out_specs=pl.BlockSpec(memory_space=pltpu.VMEM),
        scratch_shapes=[
            vmem((ROWS, NOPE), BF16),
            vmem((ROWS, ROPE), BF16),
            vmem((ROWS, NOPE), BF16),
            vmem((256, ROWS), F32),
            vmem((NY, 256, NOPE), BF16),
            vmem((NX * NZ, 16, ROWS), BF16),
            vmem((ROWS, WIDE), BF16),
            vmem((KEYS, LAT), BF16),
            vmem((WIDE, KEYS), BF16),
            vmem((64, 224, VDIM), BF16),
            vmem((64, 128, 256), BF16),
            vmem((NX, NZ, 8, VDIM), BF16),
            vmem((NY, NX, NZ, 8, VDIM), BF16),
            vmem((LAT, 256), BF16),
            vmem((WIDE, LAT), BF16),
            vmem((4, ROPE, 128), BF16),
            vmem((2, 4, LAT), BF16),
            vmem((8, ROPE), BF16),
            vmem((GROUP, KEYS), F32),
            vmem((3, GROUP, WIDE), BF16),
            vmem((NX, GROUP, WIDE), BF16),
            vmem((NZ, 16, WIDE), BF16),
            vmem((NZ, 16, WIDE), BF16),
            vmem((NX, 2, NZ * 8, 128), BF16),
            vmem((NX, 2, NZ * 8, 128), BF16),
            vmem((NZ, 8, 128), F32),
            vmem((NZ, 8, 128), F32),
            pltpu.SMEM((1,), jnp.int32),
            pltpu.SMEM((1, 4), jnp.int32),
            dma((13,)),
            dma((NY,)),
            dma((NY,)),
            dma((14,)),
            dma((14,)),
            dma((NZ,)),
            dma((NZ,)),
            dma((24,)),
            dma((24,)),
            dma((NX,)),
            dma((NX,)),
            dma((NZ,)),
            dma((NZ,)),
            dma((15,)),
            dma((15,)),
        ],
        compiler_params=pltpu.CompilerParams(
            collective_id=0, has_side_effects=True, vmem_limit_bytes=56 * 1024 * 1024
        ),
        name="latent_attention",
    )(
        prompt_lengths,
        suffix_lengths,
        query_nope.reshape(ROWS, NOPE),
        query_rope.reshape(ROWS, ROPE),
        key_map.reshape(256, NOPE),
        value_map.reshape(NX, NZ, 8, VDIM),
        out_map.reshape(64, 224, VDIM),
        prompt_latent[0],
        prompt_rope[0],
        suffix_latent.reshape(512, LAT),
        suffix_rope[0],
        new_latent[0],
        new_rope.reshape(8, ROPE),
    )
    return summed[:, :FEATS].T.astype(BF16).reshape(1, FEATS, 2, 4)


def solution(mesh):
    placed = (
        P("replica", None, None, "tensor", None),
        P("replica", None, None, "tensor", None),
        P("tensor", ("replica", "context"), None),
        P("tensor", ("replica", "context"), None),
        P(None, "tensor", "context", None),
        P("replica", "context", None),
        P("replica", None, "context"),
        P("replica"),
        P("replica", None, None, None),
        P("replica", None, None, None),
        P("replica", None),
        P("replica", None, None, None),
        P("replica", None, None, None),
    )
    return jax.shard_map(
        shards,
        mesh=mesh,
        in_specs=placed,
        out_specs=P("replica", ("context", "tensor"), None, None),
        check_vma=False,
    )
```
